512 devices in a mesh: blk: 16 (over y, x_hi, core), grp: 32 (over z, x_lo).
Axes of the slice: x: 4 (x_hi: 2, x_lo: 2; x = x_hi * 2 + x_lo), y: 4, z: 16, core: 2. Of those that a mesh axis runs over, the one named last changes fastest.
Arguments:
- factor: bfloat16 [8192, 8192], P('grp', 'blk'), may hold values from -1 to 108
- scales: float32 [64, 64], P('grp', 'blk'), may hold values from 0.5 to 2
- basis_block: bfloat16 [8192, 8192], P('grp', 'blk'), may hold values from -6 to 6
Outputs:
- new_basis: float32 [8192, 8192], P('grp', 'blk')
The draws below stay inside these ranges and needn't reach their ends.
All inputs are finite; a program needn't handle non-finite values.
Results may differ from the reference program's by a relative error of at most 0.0029.
Values may be sent and summed in bfloat16 or wider, within the bound.
A program may use at most 64 MiB of HBM per device.

```python
import math
import jax
import jax.numpy as jnp
from jax import lax

M = 8192
K = 8192
QB = 128
N_BLK = 16


def draw_factor(key, part):
    key = jax.random.fold_in(key, 11)
    key_off, key_diag = jax.random.split(key)
    off_part = jnp.clip(0.25 * jax.random.normal(key_off, (M, M), jnp.float32), -1.0, 1.0)
    factor_u = jax.random.uniform(key_diag, (M, 1), jnp.float32, 1.0, 1.5)
    row_pos = jnp.arange(M, dtype=jnp.int32)[:, None]
    col_pos = jnp.arange(M, dtype=jnp.int32)[None, :]
    factor_u = jnp.where(row_pos == M - 1, 1.5, factor_u)
    off_part = jnp.where((row_pos == 0) & (col_pos == M - 1), -1.0, off_part)
    diag_part = 24.0 * (1.0 + 2.0 * row_pos.astype(jnp.float32) / (M - 1)) * factor_u
    return jnp.where(row_pos == col_pos, diag_part, off_part).astype(jnp.bfloat16)


def steps_of(key, shape, cuts, least, largest):
    gain, own = 1.0, jax.random.fold_in(key, 6)
    for axis_at, blocks in cuts:
        heights = jnp.exp(jax.random.uniform(jax.random.fold_in(own, axis_at), (blocks,), jnp.float32, least / len(cuts), largest / len(cuts)))
        gain = gain * jnp.repeat(heights, shape[axis_at] // blocks).reshape([-1 if axis == axis_at else 1 for axis in range(len(shape))])
    return gain


def scatter_about(own_key, extent, scale, reach, pieces=(), kind=jnp.bfloat16):
    values = scale * jax.random.normal(own_key, extent, jnp.float32)
    if pieces:
        values = values * steps_of(own_key, extent, pieces, -0.22, 0.18)
    return jnp.clip(values, -reach, reach).astype(kind)


def setup_inputs(seed: int = 0) -> dict:
    key_list = jax.random.split(jax.random.key(seed), 4)
    factor = draw_factor(jax.random.fold_in(key_list[3], 71), 0)
    scales = jnp.clip(jnp.exp(math.log(2.0) - 1.3862944 * jax.random.uniform(key_list[1], (M // QB, M // QB), jnp.float32) ** steps_of(key_list[1], (M // QB, M // QB), ((0, 32), (1, 16)), -0.2, 0.2)), 0.5, 2.0)
    basis_block = scatter_about(key_list[2], (M, K), 1.0, 6.0, ((0, 32), (1, 16)))
    return dict(factor=factor, scales=scales, basis_block=basis_block)


def block_basis(pair):
    gram_block, image_block = pair
    lower_tri = jnp.linalg.cholesky(gram_block)
    inverse = jax.scipy.linalg.solve_triangular(lower_tri, jnp.eye(gram_block.shape[0], dtype=jnp.float32), lower=True)
    return jnp.dot(image_block, inverse.T, precision=lax.Precision.HIGHEST)

def reference(factor, scales, basis_block):
    nblocks = M // QB
    dequant = (factor.astype(jnp.float32).reshape(nblocks, QB, nblocks, QB) * scales[:, None, :, None]).reshape(M, M).astype(jnp.bfloat16)
    image = jnp.dot(dequant.astype(jnp.float32), basis_block.astype(jnp.float32), preferred_element_type=jnp.float32)
    stacked = jnp.transpose(image.reshape(M, N_BLK, K // N_BLK), (1, 0, 2))
    gram = jnp.einsum('bmi,bmj->bij', stacked, stacked, precision=lax.Precision.HIGHEST) / M
    result = lax.map(block_basis, (gram, stacked))
    return jnp.transpose(result, (1, 0, 2)).reshape(M, K)
```

```python
import functools

import jax
import jax.numpy as jnp
from jax import lax
from jax.experimental import pallas as pl
from jax.experimental.pallas import tpu as pltpu
from jax.sharding import PartitionSpec as P

M = 8192
NY, NX, NZ = 4, 4, 16
ROWS, COLS = 256, 512
HALF = ROWS // 2
TILE = 128
NT = COLS // TILE
PAIRS = [(i, j) for i in range(NT) for j in range(i + 1)]
PER_CORE = len(PAIRS) // 2
PIECE = TILE // NZ
SUB = 32
STEP = 4
HIGHEST = lax.Precision.HIGHEST


def dequantize(quantized, scale_block):
    row_groups, col_groups = scale_block.shape
    width = quantized.shape[0] // row_groups
    shaped = quantized.astype(jnp.float32).reshape(row_groups, width, col_groups, width)
    return (shaped * scale_block[:, None, :, None]).reshape(quantized.shape).astype(jnp.bfloat16)


def place():
    blk, grp = lax.axis_index("blk"), lax.axis_index("grp")
    core, x_hi, y = lax.rem(blk, 2), lax.rem(lax.div(blk, 2), 2), lax.div(blk, 4)
    z, x_lo = lax.div(grp, 2), lax.rem(grp, 2)
    return y, x_hi, x_lo, z, core


def device(y, x, z, core):
    return {"blk": (y * 2 + lax.div(x, 2)) * 2 + core, "grp": z * 2 + lax.rem(x, 2)}


def remote(src, dst, send, recv, to):
    return pltpu.make_async_remote_copy(
        src_ref=src, dst_ref=dst, send_sem=send, recv_sem=recv,
        device_id=to, device_id_type=pl.DeviceIdType.MESH,
    )


def gather_kernel(
    d_ref, b_ref, image_ref, gram_ref,
    d_xy, d_yx, basis, part, other, mine, arrived, total,
    own_sem, swap_s, swap_r, xy_s, xy_r, yx_s, yx_r, ring_s, ring_r, sib_s, sib_r,
    pair_s, pair_r, rs_s, rs_r, ag_s, ag_r,
):
    y, x_hi, x_lo, z, core = place()
    x = x_hi * 2 + x_lo
    sibling = device(y, x, z, 1 - core)
    partner_x = x_hi * 2 + core
    partner = device(y, partner_x, z, x_lo)
    moved = x_lo != core

    def x_peer(d):
        return device(y, lax.rem(x + d, NX), z, core)

    def y_peer(d):
        return device(lax.rem(y + d, NY), x, z, core)

    def z_peer(d):
        return device(y, x, lax.rem(z + d, NZ), core)

    barrier = pltpu.get_barrier_semaphore()

    def greet(to):
        pl.semaphore_signal(barrier, inc=1, device_id=to, device_id_type=pl.DeviceIdType.MESH)

    greet(sibling)
    for d in range(1, 4):
        greet(x_peer(d))
        greet(y_peer(d))

    @pl.loop(1, NZ)
    def _(d):
        greet(z_peer(d))

    @pl.when(moved)
    def _():
        greet(partner)
        pl.semaphore_wait(barrier, 23)

    @pl.when(jnp.logical_not(moved))
    def _():
        pl.semaphore_wait(barrier, 22)

    halves = [pl.ds(0, HALF), pl.ds(HALF, HALF)]

    @pl.when(moved)
    def _():
        sent = [
            remote(b_ref.at[halves[0]], basis.at[z, x_lo, 0], swap_s.at[0], swap_r.at[0], partner),
            remote(b_ref.at[halves[1]], basis.at[z, x_lo, 1], swap_s.at[1], swap_r.at[1], partner),
            remote(d_ref.at[halves[0]], d_xy.at[y, partner_x], swap_s.at[2], swap_r.at[2], partner),
            remote(d_ref.at[halves[1]], d_yx.at[partner_x, y], swap_s.at[3], swap_r.at[3], partner),
        ]
        for copy in sent:
            copy.start()
        for copy in sent:
            copy.wait()

    @pl.when(jnp.logical_not(moved))
    def _():
        kept = [
            pltpu.make_async_copy(b_ref.at[halves[0]], basis.at[z, core, 0], own_sem.at[0]),
            pltpu.make_async_copy(b_ref.at[halves[1]], basis.at[z, core, 1], own_sem.at[1]),
            pltpu.make_async_copy(d_ref.at[halves[0]], d_xy.at[y, x], own_sem.at[2]),
            pltpu.make_async_copy(d_ref.at[halves[1]], d_yx.at[x, y], own_sem.at[3]),
        ]
        for copy in kept:
            copy.start()
        for copy in kept:
            copy.wait()

    ways = [z_peer(1), z_peer(NZ - 1)]

    def origin(way, step):
        return lax.rem(z + (step if way else NZ - step), NZ)

    def hop(way, step, h):
        slot = basis.at[origin(way, step - 1), core, h]
        return remote(slot, slot, ring_s.at[way, step, h], ring_r.at[way, step, h], ways[way])

    def share(way, step, h):
        slot = basis.at[origin(way, step), core, h]
        return remote(slot, slot, sib_s.at[way, step, h], sib_r.at[way, step, h], sibling)

    for h in range(2):
        for way in range(2):
            hop(way, 1, h).start()
    xy_first = [remote(d_xy.at[y, x], d_xy.at[y, x], xy_s.at[d - 1], xy_r.at[d - 1], x_peer(d)) for d in (1, 3, 2)]
    yx_first = [remote(d_yx.at[x, y], d_yx.at[x, y], yx_s.at[d - 1], yx_r.at[d - 1], y_peer(d)) for d in (1, 3, 2)]
    for one, two in zip(xy_first, yx_first):
        one.start()
        two.start()
    for h in range(2):
        share(0, 0, h).start()

    def relay(step):
        for h in range(2):
            for way in range(2):
                hop(way, step, h).wait_recv()
                hop(way, step + 1, h).start()
                share(way, step, h).start()

    relay(1)
    for copy in xy_first:
        copy.wait_recv()
    for copy in yx_first:
        copy.wait_recv()
    xy_second = [remote(d_xy.at[y], d_xy.at[y], xy_s.at[d + 2], xy_r.at[d + 2], y_peer(d)) for d in (1, 3, 2)]
    yx_second = [remote(d_yx.at[x], d_yx.at[x], yx_s.at[d + 2], yx_r.at[d + 2], x_peer(d)) for d in (1, 3, 2)]
    for one, two in zip(xy_second, yx_second):
        one.start()
        two.start()

    @pl.loop(2, 7)
    def _(step):
        relay(step)

    for h in range(2):
        for way in range(2):
            hop(way, 7, h).wait_recv()
            if way == h:
                hop(way, 8, h).start()
            share(way, 7, h).start()
    for way in range(2):
        hop(way, 8, way).wait_recv()
        share(way, 8, way).start()

    for copy in xy_first + yx_first:
        copy.wait_send()
    for copy in xy_second + yx_second:
        copy.wait()
    for h in range(2):
        share(0, 0, h).wait()

    @pl.loop(1, 8)
    def _(step):
        for h in range(2):
            for way in range(2):
                hop(way, step, h).wait_send()
                share(way, step, h).wait()

    for way in range(2):
        hop(way, 8, way).wait_send()
        share(way, 8, way).wait()

    image_ref[...] = jnp.zeros_like(image_ref)

    @pl.loop(0, NZ)
    def _(k):
        ky, kx = lax.div(k, NX), lax.rem(k, NX)
        left = jnp.concatenate([d_xy[ky, kx], d_yx[kx, ky]], axis=0)
        right = basis[k].reshape(2 * ROWS, COLS)
        image_ref[...] += jnp.dot(left, right, preferred_element_type=jnp.float32)

    for q, (i, j) in enumerate(PAIRS):
        block = lax.dot_general(
            image_ref[:, i * TILE:(i + 1) * TILE], image_ref[:, j * TILE:(j + 1) * TILE],
            (((0,), (0,)), ((), ())), precision=HIGHEST, preferred_element_type=jnp.float32,
        )
        part[q // PER_CORE, :, q % PER_CORE] = block.reshape(NZ, PIECE, TILE)

    swap = remote(part.at[1 - core], other, pair_s.at[0], pair_r.at[0], sibling)
    swap.start()
    swap.wait_recv()
    mine[...] = part[core] + other[...]

    def scatter(d):
        to = lax.rem(z + d, NZ)
        return remote(mine.at[to], arrived.at[d], rs_s.at[d], rs_r.at[d], z_peer(d))

    @pl.loop(1, NZ)
    def _(d):
        scatter(d).start()

    total[core, z] = mine[z]

    @pl.loop(1, NZ)
    def _(d):
        scatter(d).wait_recv()
        total[core, z] += arrived[d]

    def spread(d):
        return remote(total.at[core, z], total.at[core, z], ag_s.at[d], ag_r.at[d], z_peer(d))

    @pl.loop(1, NZ)
    def _(d):
        spread(d).start()

    @pl.loop(1, NZ)
    def _(d):
        spread(d).wait_recv()

    both = remote(total.at[core], total.at[core], pair_s.at[1], pair_r.at[1], sibling)
    both.start()
    swap.wait_send()

    @pl.loop(1, NZ)
    def _(d):
        scatter(d).wait_send()
        spread(d).wait_send()

    both.wait()
    for q in range(len(PAIRS)):
        gram_ref[q] = total[q // PER_CORE, :, q % PER_CORE].reshape(TILE, TILE)


def tile_inverse(s_ref, v_ref, w_ref):
    shape = (SUB, TILE)
    row = lax.broadcasted_iota(jnp.int32, shape, 0)
    eye = lax.broadcasted_iota(jnp.int32, (TILE, TILE), 0) == lax.broadcasted_iota(jnp.int32, (TILE, TILE), 1)
    v_ref[...] = eye.astype(jnp.float32)
    for base in range(0, TILE, SUB):
        strip = s_ref[base:base + SUB, :]
        acts = v_ref[base:base + SUB, :]
        pivots = jnp.ones(shape, jnp.float32)
        for first in range(0, SUB, STEP):
            cols = [jnp.broadcast_to(strip[:, base + first + q:base + first + q + 1], shape) for q in range(STEP)]
            srows = [strip[first + q:first + q + 1, :] for q in range(STEP)]
            arows = [acts[first + q:first + q + 1, :] for q in range(STEP)]
            for q in range(STEP):
                at = first + q
                pivot = cols[q][at:at + 1, :]
                pivots = jnp.where(row == at, pivot, pivots)
                mult = jnp.where(row > at, cols[q] * (1.0 / pivot), 0.0)
                for r in range(q + 1, STEP):
                    cols[r] = cols[r] - mult * cols[r][at:at + 1, :]
                    factor = mult[first + r:first + r + 1, :]
                    srows[r] = srows[r] - factor * srows[q]
                    arows[r] = arows[r] - factor * arows[q]
                strip = strip - mult * srows[q]
                acts = acts - mult * arows[q]
        size = 1.0 / jnp.sqrt(pivots)
        upper = strip * size
        done = acts * size
        w_ref[base:base + SUB, :] = done
        if base + SUB < TILE:
            over = (((0,), (0,)), ((), ()))
            s_ref[...] -= lax.dot_general(upper, upper, over, precision=HIGHEST, preferred_element_type=jnp.float32)
            v_ref[...] -= lax.dot_general(upper, done, over, precision=HIGHEST, preferred_element_type=jnp.float32)


def mul(a, b, over):
    return lax.dot_general(a, b, (over, ((), ())), precision=HIGHEST, preferred_element_type=jnp.float32)


def refresh_kernel(gram_ref, image_ref, out_ref, a, l, w, s, v, wk):
    for q, (i, j) in enumerate(PAIRS):
        a[i, j] = gram_ref[q] * (1.0 / M)

    @pl.loop(0, NT)
    def _(k):
        s[...] = a[k, k]
        tile_inverse(s, v, wk)
        w[k, k] = wk[...]

        @pl.loop(k + 1, NT)
        def _(i):
            l[i, k] = mul(a[i, k], wk[...], ((1,), (1,)))

        @pl.loop(k + 1, NT)
        def _(i):
            @pl.loop(k + 1, i + 1)
            def _(j):
                a[i, j] = a[i, j] - mul(l[i, k], l[j, k], ((1,), (1,)))

    for i in range(1, NT):
        for j in range(i):
            acc = mul(l[i, j], w[j, j], ((1,), (0,)))
            for k in range(j + 1, i):
                acc = acc + mul(l[i, k], w[k, j], ((1,), (0,)))
            w[i, j] = -mul(w[i, i], acc, ((1,), (0,)))

    for i in range(NT):
        left = image_ref[:, 0:(i + 1) * TILE]
        right = jnp.concatenate([w[i, j] for j in range(i + 1)], axis=1)
        out_ref[:, i * TILE:(i + 1) * TILE] = mul(left, right, ((1,), (1,)))


def per_device(factor, scales, basis_block):
    f32, bf16, sem = jnp.float32, jnp.bfloat16, pltpu.SemaphoreType.DMA
    vmem = pl.BlockSpec(memory_space=pltpu.VMEM)
    image, gram = pl.pallas_call(
        gather_kernel,
        out_shape=(
            jax.ShapeDtypeStruct((ROWS, COLS), f32),
            jax.ShapeDtypeStruct((len(PAIRS), TILE, TILE), f32),
        ),
        in_specs=[vmem, vmem],
        out_specs=(vmem, vmem),
        scratch_shapes=[
            pltpu.VMEM((NY, NX, HALF, COLS), bf16),
            pltpu.VMEM((NX, NY, HALF, COLS), bf16),
            pltpu.VMEM((NZ, 2, 2, HALF, COLS), bf16),
            pltpu.VMEM((2, NZ, PER_CORE, PIECE, TILE), f32),
            pltpu.VMEM((NZ, PER_CORE, PIECE, TILE), f32),
            pltpu.VMEM((NZ, PER_CORE, PIECE, TILE), f32),
            pltpu.VMEM((NZ, PER_CORE, PIECE, TILE), f32),
            pltpu.VMEM((2, NZ, PER_CORE, PIECE, TILE), f32),
            sem((4,)), sem((4,)), sem((4,)),
            sem((6,)), sem((6,)), sem((6,)), sem((6,)),
            sem((2, 9, 2)), sem((2, 9, 2)), sem((2, 9, 2)), sem((2, 9, 2)),
            sem((2,)), sem((2,)),
            sem((NZ,)), sem((NZ,)), sem((NZ,)), sem((NZ,)),
        ],
        compiler_params=pltpu.CompilerParams(
            collective_id=0, has_side_effects=True, vmem_limit_bytes=48 * 2**20
        ),
        name="gather_gram",
    )(dequantize(factor, scales), basis_block)
    tile = pltpu.VMEM((TILE, TILE), f32)
    tiles = pltpu.VMEM((NT, NT, TILE, TILE), f32)
    result = pl.pallas_call(
        refresh_kernel,
        out_shape=jax.ShapeDtypeStruct((ROWS, COLS), f32),
        in_specs=[vmem, vmem],
        out_specs=vmem,
        scratch_shapes=[tiles, tiles, tiles, tile, tile, tile],
        compiler_params=pltpu.CompilerParams(vmem_limit_bytes=32 * 2**20),
        name="refresh",
    )(gram, image)
    pairs = []
    for rest in range(8):
        for z in range(NZ):
            one, two = (rest * 2 + 1) * 32 + z * 2, (rest * 2) * 32 + z * 2 + 1
            pairs += [(one, two), (two, one)]
    back = lax.ppermute(result, ("blk", "grp"), pairs)
    _, _, x_lo, _, core = place()
    return jnp.where(x_lo == core, result, back)


def solution(mesh):
    return jax.shard_map(
        per_device,
        mesh=mesh,
        in_specs=(P("grp", "blk"), P("grp", "blk"), P("grp", "blk")),
        out_specs=P("grp", "blk"),
        check_vma=False,
    )
```

```python
import jax
import jax.numpy as jnp
from jax import lax
from jax.experimental import pallas as pl
from jax.experimental.pallas import tpu as pltpu
from jax.sharding import PartitionSpec as P

M = 8192
NY, NX, NZ = 4, 4, 16
ROWS, COLS = 256, 512
HALF = ROWS // 2
TILE = 128
NT = COLS // TILE
PAIRS = [(i, j) for i in range(NT) for j in range(i + 1)]
PER_CORE = len(PAIRS) // 2
PIECE = TILE // NZ
SUB = 32
STEP = 4
HIGHEST = lax.Precision.HIGHEST


def dequantize(quantized, scale_block):
    row_groups, col_groups = scale_block.shape
    width = quantized.shape[0] // row_groups
    shaped = quantized.astype(jnp.float32).reshape(row_groups, width, col_groups, width)
    return (shaped * scale_block[:, None, :, None]).reshape(quantized.shape).astype(jnp.bfloat16)


def place():
    blk, grp = lax.axis_index("blk"), lax.axis_index("grp")
    core, x_hi, y = lax.rem(blk, 2), lax.rem(lax.div(blk, 2), 2), lax.div(blk, 4)
    z, x_lo = lax.div(grp, 2), lax.rem(grp, 2)
    return y, x_hi, x_lo, z, core


def device(y, x, z, core):
    return {"blk": (y * 2 + lax.div(x, 2)) * 2 + core, "grp": z * 2 + lax.rem(x, 2)}


def remote(src, dst, send, recv, to):
    return pltpu.make_async_remote_copy(
        src_ref=src, dst_ref=dst, send_sem=send, recv_sem=recv,
        device_id=to, device_id_type=pl.DeviceIdType.MESH,
    )


def gather_kernel(
    d_ref, b_ref, image_ref, gram_ref,
    d_xy, d_yx, basis, image, image_in, part, other, mine, near, far, summed, total,
    own_sem, swap_s, swap_r, xy_s, xy_r, yx_s, yx_r, ring_s, ring_r, sib_s, sib_r,
    pair_s, pair_r, rs_s, rs_r, ag_s, ag_r, across_s, across_r,
):
    y, x_hi, x_lo, z, core = place()
    x = x_hi * 2 + x_lo
    sibling = device(y, x, z, 1 - core)
    partner_x = x_hi * 2 + core
    partner = device(y, partner_x, z, x_lo)
    moved = x_lo != core
    twin = device(y, x_hi * 2 + 1 - x_lo, z, core)

    def x_peer(d):
        return device(y, lax.rem(x + d, NX), z, core)

    def y_peer(d):
        return device(lax.rem(y + d, NY), x, z, core)

    def z_peer(d):
        return device(y, x, lax.rem(z + d, NZ), core)

    barrier = pltpu.get_barrier_semaphore()

    def greet(to):
        pl.semaphore_signal(barrier, inc=1, device_id=to, device_id_type=pl.DeviceIdType.MESH)

    greet(sibling)
    for d in range(1, 4):
        greet(x_peer(d))
        greet(y_peer(d))
    for d in (1, 15, 2, 14, 4, 8, 12):
        greet(z_peer(d))

    @pl.when(moved)
    def _():
        greet(partner)
        pl.semaphore_wait(barrier, 15)

    @pl.when(jnp.logical_not(moved))
    def _():
        pl.semaphore_wait(barrier, 14)

    halves = [pl.ds(0, HALF), pl.ds(HALF, HALF)]

    @pl.when(moved)
    def _():
        sent = [
            remote(b_ref.at[halves[0]], basis.at[z, x_lo, 0], swap_s.at[0], swap_r.at[0], partner),
            remote(b_ref.at[halves[1]], basis.at[z, x_lo, 1], swap_s.at[1], swap_r.at[1], partner),
            remote(d_ref.at[halves[0]], d_xy.at[y, partner_x], swap_s.at[2], swap_r.at[2], partner),
            remote(d_ref.at[halves[1]], d_yx.at[partner_x, y], swap_s.at[3], swap_r.at[3], partner),
        ]
        for copy in sent:
            copy.start()
        for copy in sent:
            copy.wait()

    @pl.when(jnp.logical_not(moved))
    def _():
        kept = [
            pltpu.make_async_copy(b_ref.at[halves[0]], basis.at[z, core, 0], own_sem.at[0]),
            pltpu.make_async_copy(b_ref.at[halves[1]], basis.at[z, core, 1], own_sem.at[1]),
            pltpu.make_async_copy(d_ref.at[halves[0]], d_xy.at[y, x], own_sem.at[2]),
            pltpu.make_async_copy(d_ref.at[halves[1]], d_yx.at[x, y], own_sem.at[3]),
        ]
        for copy in kept:
            copy.start()
        for copy in kept:
            copy.wait()

    ways = [z_peer(1), z_peer(NZ - 1)]

    def origin(way, step):
        return lax.rem(z + (step if way else NZ - step), NZ)

    def hop(way, step, h):
        slot = basis.at[origin(way, step - 1), core, h]
        return remote(slot, slot, ring_s.at[way, step, h], ring_r.at[way, step, h], ways[way])

    def share(way, step, h):
        slot = basis.at[origin(way, step), core, h]
        return remote(slot, slot, sib_s.at[way, step, h], sib_r.at[way, step, h], sibling)

    for h in range(2):
        for way in range(2):
            hop(way, 1, h).start()
    xy_first = [remote(d_xy.at[y, x], d_xy.at[y, x], xy_s.at[d - 1], xy_r.at[d - 1], x_peer(d)) for d in (1, 3, 2)]
    yx_first = [remote(d_yx.at[x, y], d_yx.at[x, y], yx_s.at[d - 1], yx_r.at[d - 1], y_peer(d)) for d in (1, 3, 2)]
    for one, two in zip(xy_first, yx_first):
        one.start()
        two.start()
    for h in range(2):
        share(0, 0, h).start()

    def relay(step):
        for h in range(2):
            for way in range(2):
                hop(way, step, h).wait_recv()
                hop(way, step + 1, h).start()
                share(way, step, h).start()

    relay(1)
    for copy in xy_first:
        copy.wait_recv()
    for copy in yx_first:
        copy.wait_recv()
    xy_second = [remote(d_xy.at[y], d_xy.at[y], xy_s.at[d + 2], xy_r.at[d + 2], y_peer(d)) for d in (1, 3, 2)]
    yx_second = [remote(d_yx.at[x], d_yx.at[x], yx_s.at[d + 2], yx_r.at[d + 2], x_peer(d)) for d in (1, 3, 2)]
    for one, two in zip(xy_second, yx_second):
        one.start()
        two.start()

    image[...] = jnp.zeros_like(image)

    @pl.loop(2, 6)
    def _(step):
        relay(step)

    for copy in xy_second + yx_second:
        copy.wait_recv()

    def product(k):
        ky, kx = lax.div(k, NX), lax.rem(k, NX)
        left = jnp.concatenate([d_xy[ky, kx], d_yx[kx, ky]], axis=0)
        right = basis[k].reshape(2 * ROWS, COLS)
        return jnp.dot(left, right, preferred_element_type=jnp.float32)

    def multiply(first, end):
        @pl.loop(first, end)
        def _(step):
            for h in range(2):
                for way in range(2):
                    share(way, step, h).wait_recv()
            image[...] += product(origin(0, step)) + product(origin(1, step))

    for h in range(2):
        share(0, 0, h).wait_recv()
    image[...] += product(z)
    multiply(1, 2)
    relay(6)
    multiply(2, 5)
    for h in range(2):
        for way in range(2):
            hop(way, 7, h).wait_recv()
            if way == h:
                hop(way, 8, h).start()
            share(way, 7, h).start()
    multiply(5, 7)
    for way in range(2):
        hop(way, 8, way).wait_recv()
        share(way, 8, way).start()
    multiply(7, 8)
    for way in range(2):
        share(way, 8, way).wait_recv()
    image[...] += product(origin(0, 8))

    send_image = remote(image, image_in, swap_s.at[4], swap_r.at[4], partner)

    @pl.when(moved)
    def _():
        send_image.start()

    for top in (0, 2):
        width = (top + 2) * TILE
        block = lax.dot_general(
            image[:, top * TILE:width], image[:, 0:width],
            (((0,), (0,)), ((), ())), precision=HIGHEST, preferred_element_type=jnp.float32,
        )
        for q, (i, j) in enumerate(PAIRS):
            if top <= i < top + 2:
                for t in range(NZ):
                    at = (i - top) * TILE + t * PIECE
                    part[q // PER_CORE, t % 4, t // 4, q % PER_CORE] = block[at:at + PIECE, j * TILE:(j + 1) * TILE]

    swap = remote(part.at[1 - core], other, pair_s.at[0], pair_r.at[0], sibling)
    swap.start()
    z_q, z_r = lax.div(z, 4), lax.rem(z, 4)
    offsets = (0, 1, NZ - 1, lax.rem(2 + 12 * core, NZ))
    swap.wait_recv()
    mine[...] = part[core] + other[...]
    to_near = [
        remote(mine.at[lax.rem(z_r + offsets[n], 4)], near.at[n], rs_s.at[n], rs_r.at[n], z_peer(offsets[n]))
        for n in (1, 2, 3)
    ]
    for copy in to_near:
        copy.start()
    for copy in to_near:
        copy.wait_recv()
    near[0] = mine[z_r] + near[1] + near[2] + near[3]
    to_far = [
        remote(near.at[0, lax.rem(z_q + d, 4)], far.at[d], rs_s.at[3 + d], rs_r.at[3 + d], z_peer(4 * d))
        for d in (1, 2, 3)
    ]
    for copy in to_far:
        copy.start()
    for copy in to_far:
        copy.wait_recv()
    summed[...] = near[0, z_q] + far[1] + far[2] + far[3]

    hand = remote(summed, total.at[core, z_r, z_q], swap_s.at[5], swap_r.at[5], partner)

    @pl.when(moved)
    def _():
        hand.start()
        hand.wait_recv()

    @pl.when(jnp.logical_not(moved))
    def _():
        total[core, z_r, z_q] = summed[...]

    own = total.at[x_lo, z_r, z_q]
    spread_far = [remote(own, own, ag_s.at[d], ag_r.at[d], z_peer(4 * d)) for d in (1, 2, 3)]
    for copy in spread_far:
        copy.start()
    for copy in spread_far:
        copy.wait_recv()
    group = total.at[x_lo, z_r]
    spread_near = [
        remote(group, group, ag_s.at[3 + n], ag_r.at[3 + n], z_peer(offsets[n])) for n in (1, 2, 3)
    ]
    for copy in spread_near:
        copy.start()

    def cross(n):
        slot = total.at[x_lo, lax.rem(z_r + NZ - offsets[n], 4)]
        return remote(slot, slot, across_s.at[n], across_r.at[n], twin)

    crossing = [cross(n) for n in range(4)]
    crossing[0].start()
    for n in (1, 2, 3):
        spread_near[n - 1].wait_recv()
        crossing[n].start()

    for copy in xy_first + yx_first + xy_second + yx_second:
        copy.wait_send()
    for h in range(2):
        share(0, 0, h).wait_send()

    @pl.loop(1, 8)
    def _(step):
        for h in range(2):
            for way in range(2):
                hop(way, step, h).wait_send()
                share(way, step, h).wait_send()

    for way in range(2):
        hop(way, 8, way).wait_send()
        share(way, 8, way).wait_send()
    swap.wait_send()
    for copy in to_near + to_far + spread_far + spread_near:
        copy.wait_send()

    @pl.when(moved)
    def _():
        hand.wait_send()
        send_image.wait()
        image_ref[...] = image_in[...]

    @pl.when(jnp.logical_not(moved))
    def _():
        image_ref[...] = image[...]

    for copy in crossing:
        copy.wait()
    for q in range(len(PAIRS)):
        for t in range(NZ):
            gram_ref[q, t * PIECE:(t + 1) * PIECE, :] = total[q // PER_CORE, t % 4, t // 4, q % PER_CORE]


def tile_inverse(s_ref, v_ref, w_ref):
    vreg = (8, TILE)
    groups = SUB // 8
    row = lax.broadcasted_iota(jnp.int32, vreg, 0)
    eye = lax.broadcasted_iota(jnp.int32, (TILE, TILE), 0) == lax.broadcasted_iota(jnp.int32, (TILE, TILE), 1)
    v_ref[...] = eye.astype(jnp.float32)
    spread = lambda value: jnp.broadcast_to(value, vreg)
    for base in range(0, TILE, SUB):
        strip = [s_ref[base + 8 * g:base + 8 * g + 8, :] for g in range(groups)]
        acts = [v_ref[base + 8 * g:base + 8 * g + 8, :] for g in range(groups)]
        pivots = [jnp.ones(vreg, jnp.float32) for _ in range(groups)]
        for first in range(0, SUB, STEP):
            g0, r0, c0 = first // 8, first % 8, base + first
            live = range(g0, groups)
            srows = [spread(strip[g0][r0 + q:r0 + q + 1, :]) for q in range(STEP)]
            arows = [spread(acts[g0][r0 + q:r0 + q + 1, :]) for q in range(STEP)]
            cols = [{g: spread(strip[g][:, c0 + q:c0 + q + 1]) for g in live} for q in range(STEP)]
            block = {
                (q, r): spread(srows[q][:, c0 + r:c0 + r + 1]) for q in range(STEP) for r in range(q, STEP)
            }
            for q in range(STEP):
                inv = 1.0 / block[q, q]
                pivots[g0] = jnp.where(row == r0 + q, block[q, q], pivots[g0])
                factor = {r: block[q, r] * inv for r in range(q + 1, STEP)}
                for r in range(q + 1, STEP):
                    for t in range(r, STEP):
                        block[r, t] = block[r, t] - factor[r] * block[q, t]
                for g in live:
                    mult = cols[q][g] * inv
                    for r in range(q + 1, STEP):
                        cols[r][g] = cols[r][g] - mult * block[q, r]
                    if g == g0:
                        mult = jnp.where(row > r0 + q, mult, 0.0)
                    strip[g] = strip[g] - mult * srows[q]
                    acts[g] = acts[g] - mult * arows[q]
                for r in range(q + 1, STEP):
                    srows[r] = srows[r] - factor[r] * srows[q]
                    arows[r] = arows[r] - factor[r] * arows[q]
        size = [1.0 / jnp.sqrt(p) for p in pivots]
        upper = jnp.concatenate([s * n for s, n in zip(strip, size)], axis=0)
        done = jnp.concatenate([s * n for s, n in zip(acts, size)], axis=0)
        w_ref[base:base + SUB, :] = done
        below = base + SUB
        if below < TILE:
            s_ref[below:, :] -= mul(upper[:, below:], upper, ((0,), (0,)))
            v_ref[below:, :] -= mul(upper[:, below:], done, ((0,), (0,)))


def mul(a, b, over):
    return lax.dot_general(a, b, (over, ((), ())), precision=HIGHEST, preferred_element_type=jnp.float32)


def refresh_kernel(gram_ref, image_ref, out_ref, a, w, v, s, vt):
    for q, (i, j) in enumerate(PAIRS):
        a[i * TILE:(i + 1) * TILE, j * TILE:(j + 1) * TILE] = gram_ref[q] * (1.0 / M)

    for k in range(NT):
        k0, k1 = k * TILE, (k + 1) * TILE
        s[...] = a[k0:k1, k0:k1]
        tile_inverse(s, vt, w.at[k0:k1, k0:k1])
        wk = w[k0:k1, k0:k1]
        if k < NT - 1:
            panel = mul(a[k1:, k0:k1], wk, ((1,), (1,)))
            for j in range(k + 1, NT):
                j0, j1 = j * TILE, (j + 1) * TILE
                a[j0:, j0:j1] -= mul(panel[j0 - k1:], panel[j0 - k1:j1 - k1], ((1,), (1,)))
        if k > 0:
            w[k0:k1, 0:k0] = mul(wk, v[k0:k1, 0:k0], ((1,), (0,)))
        if k < NT - 1:
            v[k1:, k0:k1] = -mul(panel, wk, ((1,), (0,)))
            if k > 0:
                v[k1:, 0:k0] -= mul(panel, w[k0:k1, 0:k0], ((1,), (0,)))
        out_ref[:, k0:k1] = mul(image_ref[:, 0:k1], w[k0:k1, 0:k1], ((1,), (1,)))


def per_device(factor, scales, basis_block):
    f32, bf16, sem = jnp.float32, jnp.bfloat16, pltpu.SemaphoreType.DMA
    vmem = pl.BlockSpec(memory_space=pltpu.VMEM)
    image, gram = pl.pallas_call(
        gather_kernel,
        out_shape=(
            jax.ShapeDtypeStruct((ROWS, COLS), f32),
            jax.ShapeDtypeStruct((len(PAIRS), TILE, TILE), f32),
        ),
        in_specs=[vmem, vmem],
        out_specs=(vmem, vmem),
        scratch_shapes=[
            pltpu.VMEM((NY, NX, HALF, COLS), bf16),
            pltpu.VMEM((NX, NY, HALF, COLS), bf16),
            pltpu.VMEM((NZ, 2, 2, HALF, COLS), bf16),
            pltpu.VMEM((ROWS, COLS), f32),
            pltpu.VMEM((ROWS, COLS), f32),
            pltpu.VMEM((2, 4, 4, PER_CORE, PIECE, TILE), f32),
            pltpu.VMEM((4, 4, PER_CORE, PIECE, TILE), f32),
            pltpu.VMEM((4, 4, PER_CORE, PIECE, TILE), f32),
            pltpu.VMEM((4, 4, PER_CORE, PIECE, TILE), f32),
            pltpu.VMEM((4, PER_CORE, PIECE, TILE), f32),
            pltpu.VMEM((PER_CORE, PIECE, TILE), f32),
            pltpu.VMEM((2, 4, 4, PER_CORE, PIECE, TILE), f32),
            sem((4,)), sem((6,)), sem((6,)),
            sem((6,)), sem((6,)), sem((6,)), sem((6,)),
            sem((2, 9, 2)), sem((2, 9, 2)), sem((2, 9, 2)), sem((2, 9, 2)),
            sem((1,)), sem((1,)),
            sem((7,)), sem((7,)), sem((7,)), sem((7,)),
            sem((4,)), sem((4,)),
        ],
        compiler_params=pltpu.CompilerParams(
            collective_id=0, has_side_effects=True, vmem_limit_bytes=48 * 2**20
        ),
        name="gather_gram",
    )(dequantize(factor, scales), basis_block)
    tile = pltpu.VMEM((TILE, TILE), f32)
    square = pltpu.VMEM((COLS, COLS), f32)
    return pl.pallas_call(
        refresh_kernel,
        out_shape=jax.ShapeDtypeStruct((ROWS, COLS), f32),
        in_specs=[vmem, vmem],
        out_specs=vmem,
        scratch_shapes=[square, square, square, tile, tile],
        compiler_params=pltpu.CompilerParams(vmem_limit_bytes=32 * 2**20),
        name="refresh",
    )(gram, image)


def solution(mesh):
    return jax.shard_map(
        per_device,
        mesh=mesh,
        in_specs=(P("grp", "blk"), P("grp", "blk"), P("grp", "blk")),
        out_specs=P("grp", "blk"),
        check_vma=False,
    )
```

```python
import jax
import jax.numpy as jnp
from jax import lax
from jax.experimental import pallas as pl
from jax.experimental.pallas import tpu as pltpu
from jax.sharding import PartitionSpec as P

M = 8192
NY, NX, NZ = 4, 4, 16
ROWS, COLS = 256, 512
HALF = ROWS // 2
TILE = 128
NT = COLS // TILE
PAIRS = [(i, j) for i in range(NT) for j in range(i + 1)]
PER_CORE = len(PAIRS) // 2
PIECE = TILE // NZ
SUB = 64
STEP = 4
HIGHEST = lax.Precision.HIGHEST


def place():
    blk, grp = lax.axis_index("blk"), lax.axis_index("grp")
    core, x_hi, y = lax.rem(blk, 2), lax.rem(lax.div(blk, 2), 2), lax.div(blk, 4)
    z, x_lo = lax.div(grp, 2), lax.rem(grp, 2)
    return y, x_hi, x_lo, z, core


def device(y, x, z, core):
    return {"blk": (y * 2 + lax.div(x, 2)) * 2 + core, "grp": z * 2 + lax.rem(x, 2)}


def remote(src, dst, send, recv, to):
    return pltpu.make_async_remote_copy(
        src_ref=src, dst_ref=dst, send_sem=send, recv_sem=recv,
        device_id=to, device_id_type=pl.DeviceIdType.MESH,
    )


def gather_kernel(
    f_ref, scale_ref, b_ref, image_ref, gram_ref,
    f_in, dequant, d_xy, d_yx, basis, image, image_in, part, other, mine, near, far, summed, total,
    own_sem, swap_s, swap_r, xy_s, xy_r, yx_s, yx_r, ring_s, ring_r, sib_s, sib_r,
    pair_s, pair_r, rs_s, rs_r, ag_s, ag_r, across_s, across_r,
):
    y, x_hi, x_lo, z, core = place()
    x = x_hi * 2 + x_lo
    sibling = device(y, x, z, 1 - core)
    partner_x = x_hi * 2 + core
    partner = device(y, partner_x, z, x_lo)
    moved = x_lo != core
    twin = device(y, x_hi * 2 + 1 - x_lo, z, core)

    def x_peer(d):
        return device(y, lax.rem(x + d, NX), z, core)

    def y_peer(d):
        return device(lax.rem(y + d, NY), x, z, core)

    def z_peer(d):
        return device(y, x, lax.rem(z + d, NZ), core)

    load = pltpu.make_async_copy(f_ref, f_in, own_sem.at[4])
    load.start()
    barrier = pltpu.get_barrier_semaphore()

    def greet(to):
        pl.semaphore_signal(barrier, inc=1, device_id=to, device_id_type=pl.DeviceIdType.MESH)

    greet(sibling)
    for d in range(1, 4):
        greet(x_peer(d))
        greet(y_peer(d))
    for d in (1, 15, 2, 14, 4, 8, 12):
        greet(z_peer(d))

    @pl.when(moved)
    def _():
        greet(partner)

    load.wait()
    for i in range(ROWS // TILE):
        for j in range(NT):
            at = (slice(i * TILE, (i + 1) * TILE), slice(j * TILE, (j + 1) * TILE))
            dequant[at] = (f_in[at].astype(jnp.float32) * scale_ref[i, j]).astype(jnp.bfloat16)

    @pl.when(moved)
    def _():
        pl.semaphore_wait(barrier, 15)

    @pl.when(jnp.logical_not(moved))
    def _():
        pl.semaphore_wait(barrier, 14)

    halves = [pl.ds(0, HALF), pl.ds(HALF, HALF)]
    swap_b = [
        remote(b_ref.at[halves[h]], basis.at[z, x_lo, h], swap_s.at[h], swap_r.at[h], partner) for h in range(2)
    ]
    swap_d = [
        remote(dequant.at[halves[0]], d_xy.at[y, partner_x], swap_s.at[2], swap_r.at[2], partner),
        remote(dequant.at[halves[1]], d_yx.at[partner_x, y], swap_s.at[3], swap_r.at[3], partner),
    ]
    kept_b = [pltpu.make_async_copy(b_ref.at[halves[h]], basis.at[z, core, h], own_sem.at[h]) for h in range(2)]
    kept_d = [
        pltpu.make_async_copy(dequant.at[halves[0]], d_xy.at[y, x], own_sem.at[2]),
        pltpu.make_async_copy(dequant.at[halves[1]], d_yx.at[x, y], own_sem.at[3]),
    ]

    @pl.when(moved)
    def _():
        for copy in swap_b:
            copy.start()
        for copy in swap_b:
            copy.wait()
        for copy in swap_d:
            copy.start()

    @pl.when(jnp.logical_not(moved))
    def _():
        for copy in kept_b + kept_d:
            copy.start()
        for copy in kept_b:
            copy.wait()

    ways = [z_peer(1), z_peer(NZ - 1)]

    def origin(way, step):
        return lax.rem(z + (step if way else NZ - step), NZ)

    def hop(way, step, h):
        slot = basis.at[origin(way, step - 1), core, h]
        return remote(slot, slot, ring_s.at[way, step, h], ring_r.at[way, step, h], ways[way])

    def share(way, step, h):
        slot = basis.at[origin(way, step), core, h]
        return remote(slot, slot, sib_s.at[way, step, h], sib_r.at[way, step, h], sibling)

    for h in range(2):
        for way in range(2):
            hop(way, 1, h).start()
    for h in range(2):
        share(0, 0, h).start()

    @pl.when(moved)
    def _():
        for copy in swap_d:
            copy.wait()

    @pl.when(jnp.logical_not(moved))
    def _():
        for copy in kept_d:
            copy.wait()

    def both_ways(refs, send, recv, to):
        return [remote(refs[n], refs[n], send.at[n], recv.at[n], to[n]) for n in (0, 1)]

    x_next, y_next = [x_peer(1), x_peer(NX - 1)], [y_peer(1), y_peer(NY - 1)]
    x_back, x_on = lax.rem(x + NX - 1, NX), lax.rem(x + 1, NX)
    y_back, y_on = lax.rem(y + NY - 1, NY), lax.rem(y + 1, NY)
    quarter = [pl.ds(0, HALF // 2), pl.ds(HALF // 2, HALF // 2)]
    pair = [pl.ds(0, 2), pl.ds(2, 2)]
    first = (
        both_ways([d_xy.at[y, x]] * 2, xy_s.at[0], xy_r.at[0], x_next)
        + both_ways([d_yx.at[x, y]] * 2, yx_s.at[0], yx_r.at[0], y_next)
    )
    first_on = (
        both_ways([d_xy.at[y, x_back, quarter[0]], d_xy.at[y, x_on, quarter[1]]], xy_s.at[1], xy_r.at[1], x_next)
        + both_ways([d_yx.at[x, y_back, quarter[0]], d_yx.at[x, y_on, quarter[1]]], yx_s.at[1], yx_r.at[1], y_next)
    )
    second = (
        both_ways([d_xy.at[y]] * 2, xy_s.at[2], xy_r.at[2], y_next)
        + both_ways([d_yx.at[x]] * 2, yx_s.at[2], yx_r.at[2], x_next)
    )
    second_on = (
        both_ways([d_xy.at[y_back, pair[0]], d_xy.at[y_on, pair[1]]], xy_s.at[3], xy_r.at[3], y_next)
        + both_ways([d_yx.at[x_back, pair[0]], d_yx.at[x_on, pair[1]]], yx_s.at[3], yx_r.at[3], x_next)
    )

    def start(copies):
        for copy in copies:
            copy.start()

    def land(copies):
        for copy in copies:
            copy.wait_recv()

    start(first)

    def relay(step):
        for h in range(2):
            for way in range(2):
                hop(way, step, h).wait_recv()
                hop(way, step + 1, h).start()
                share(way, step, h).start()

    relay(1)
    land(first)
    start(first_on)
    relay(2)
    land(first_on)
    start(second)
    image[...] = jnp.zeros_like(image)
    relay(3)
    relay(4)
    land(second)
    start(second_on)
    relay(5)
    relay(6)
    land(second_on)

    def product(k):
        ky, kx = lax.div(k, NX), lax.rem(k, NX)
        left = jnp.concatenate([d_xy[ky, kx], d_yx[kx, ky]], axis=0)
        right = basis[k].reshape(2 * ROWS, COLS)
        return jnp.dot(left, right, preferred_element_type=jnp.float32)

    def multiply(first, end):
        @pl.loop(first, end)
        def _(step):
            for h in range(2):
                for way in range(2):
                    share(way, step, h).wait_recv()
            image[...] += product(origin(0, step)) + product(origin(1, step))

    for h in range(2):
        share(0, 0, h).wait_recv()
    image[...] += product(z)
    multiply(1, 3)
    for h in range(2):
        for way in range(2):
            hop(way, 7, h).wait_recv()
            if way == h:
                hop(way, 8, h).start()
            share(way, 7, h).start()
    multiply(3, 6)
    for way in range(2):
        hop(way, 8, way).wait_recv()
        share(way, 8, way).start()
    multiply(6, 8)
    for way in range(2):
        share(way, 8, way).wait_recv()
    image[...] += product(origin(0, 8))

    send_image = remote(image, image_in, swap_s.at[4], swap_r.at[4], partner)

    @pl.when(moved)
    def _():
        send_image.start()

    for top in (0, 2):
        width = (top + 2) * TILE
        block = lax.dot_general(
            image[:, top * TILE:width], image[:, 0:width],
            (((0,), (0,)), ((), ())), precision=HIGHEST, preferred_element_type=jnp.float32,
        )
        for q, (i, j) in enumerate(PAIRS):
            if top <= i < top + 2:
                for t in range(NZ):
                    at = (i - top) * TILE + t * PIECE
                    part[q // PER_CORE, t % 4, t // 4, q % PER_CORE] = block[at:at + PIECE, j * TILE:(j + 1) * TILE]

    swap = remote(part.at[1 - core], other, pair_s.at[0], pair_r.at[0], sibling)
    swap.start()
    z_q, z_r = lax.div(z, 4), lax.rem(z, 4)
    offsets = (0, 1, NZ - 1, lax.rem(2 + 12 * core, NZ))
    swap.wait_recv()
    mine[...] = part[core] + other[...]
    to_near = [
        remote(mine.at[lax.rem(z_r + offsets[n], 4)], near.at[n], rs_s.at[n], rs_r.at[n], z_peer(offsets[n]))
        for n in (1, 2, 3)
    ]
    for copy in to_near:
        copy.start()
    for copy in to_near:
        copy.wait_recv()
    near[0] = mine[z_r] + near[1] + near[2] + near[3]
    to_far = [
        remote(near.at[0, lax.rem(z_q + d, 4)], far.at[d], rs_s.at[3 + d], rs_r.at[3 + d], z_peer(4 * d))
        for d in (1, 2, 3)
    ]
    for copy in to_far:
        copy.start()
    for copy in to_far:
        copy.wait_recv()
    summed[...] = near[0, z_q] + far[1] + far[2] + far[3]

    hand = remote(summed, total.at[core, z_r, z_q], swap_s.at[5], swap_r.at[5], partner)

    @pl.when(moved)
    def _():
        hand.start()
        hand.wait_recv()

    @pl.when(jnp.logical_not(moved))
    def _():
        total[core, z_r, z_q] = summed[...]

    own = total.at[x_lo, z_r, z_q]
    spread_far = [remote(own, own, ag_s.at[d], ag_r.at[d], z_peer(4 * d)) for d in (1, 2, 3)]
    for copy in spread_far:
        copy.start()
    for copy in spread_far:
        copy.wait_recv()
    group = total.at[x_lo, z_r]
    spread_near = [
        remote(group, group, ag_s.at[3 + n], ag_r.at[3 + n], z_peer(offsets[n])) for n in (1, 2, 3)
    ]
    for copy in spread_near:
        copy.start()

    def cross(n):
        slot = total.at[x_lo, lax.rem(z_r + NZ - offsets[n], 4)]
        return remote(slot, slot, across_s.at[n], across_r.at[n], twin)

    crossing = [cross(n) for n in range(4)]
    crossing[0].start()
    for n in (1, 2, 3):
        spread_near[n - 1].wait_recv()
        crossing[n].start()

    for copy in first + first_on + second + second_on:
        copy.wait_send()
    for h in range(2):
        share(0, 0, h).wait_send()

    @pl.loop(1, 8)
    def _(step):
        for h in range(2):
            for way in range(2):
                hop(way, step, h).wait_send()
                share(way, step, h).wait_send()

    for way in range(2):
        hop(way, 8, way).wait_send()
        share(way, 8, way).wait_send()
    swap.wait_send()
    for copy in to_near + to_far + spread_far + spread_near:
        copy.wait_send()

    @pl.when(moved)
    def _():
        hand.wait_send()
        send_image.wait()
        image_ref[...] = image_in[...]

    @pl.when(jnp.logical_not(moved))
    def _():
        image_ref[...] = image[...]

    for copy in crossing:
        copy.wait()
    for q in range(len(PAIRS)):
        for t in range(NZ):
            gram_ref[q, t * PIECE:(t + 1) * PIECE, :] = total[q // PER_CORE, t % 4, t // 4, q % PER_CORE]


def tile_inverse(s_ref, v_ref, w_ref):
    vreg = (8, TILE)
    groups = SUB // 8
    row = lax.broadcasted_iota(jnp.int32, vreg, 0)
    eye = lax.broadcasted_iota(jnp.int32, (TILE, TILE), 0) == lax.broadcasted_iota(jnp.int32, (TILE, TILE), 1)
    v_ref[...] = eye.astype(jnp.float32)
    spread = lambda value: jnp.broadcast_to(value, vreg)
    for base in range(0, TILE, SUB):
        strip = [s_ref[base + 8 * g:base + 8 * g + 8, :] for g in range(groups)]
        acts = [v_ref[base + 8 * g:base + 8 * g + 8, :] for g in range(groups)]
        pivots = [jnp.ones(vreg, jnp.float32) for _ in range(groups)]
        for first in range(0, SUB, STEP):
            g0, r0, c0 = first // 8, first % 8, base + first
            live = range(g0, groups)
            srows = [spread(strip[g0][r0 + q:r0 + q + 1, :]) for q in range(STEP)]
            arows = [spread(acts[g0][r0 + q:r0 + q + 1, :]) for q in range(STEP)]
            cols = [{g: spread(strip[g][:, c0 + q:c0 + q + 1]) for g in live} for q in range(STEP)]
            block = {
                (q, r): spread(srows[q][:, c0 + r:c0 + r + 1]) for q in range(STEP) for r in range(q, STEP)
            }
            for q in range(STEP):
                inv = 1.0 / block[q, q]
                pivots[g0] = jnp.where(row == r0 + q, block[q, q], pivots[g0])
                factor = {r: block[q, r] * inv for r in range(q + 1, STEP)}
                for r in range(q + 1, STEP):
                    for t in range(r, STEP):
                        block[r, t] = block[r, t] - factor[r] * block[q, t]
                for g in live:
                    mult = cols[q][g] * inv
                    for r in range(q + 1, STEP):
                        cols[r][g] = cols[r][g] - mult * block[q, r]
                    if g == g0:
                        mult = jnp.where(row > r0 + q, mult, 0.0)
                    strip[g] = strip[g] - mult * srows[q]
                    acts[g] = acts[g] - mult * arows[q]
                for r in range(q + 1, STEP):
                    srows[r] = srows[r] - factor[r] * srows[q]
                    arows[r] = arows[r] - factor[r] * arows[q]
        size = [1.0 / jnp.sqrt(p) for p in pivots]
        upper = jnp.concatenate([s * n for s, n in zip(strip, size)], axis=0)
        done = jnp.concatenate([s * n for s, n in zip(acts, size)], axis=0)
        w_ref[base:base + SUB, :] = done
        below = base + SUB
        if below < TILE:
            s_ref[below:, :] -= mul(upper[:, below:], upper, ((0,), (0,)))
            v_ref[below:, :] -= mul(upper[:, below:], done, ((0,), (0,)))


def mul(a, b, over):
    return lax.dot_general(a, b, (over, ((), ())), precision=HIGHEST, preferred_element_type=jnp.float32)


def refresh_kernel(gram_ref, image_ref, out_ref, a, w, v, s, vt):
    for q, (i, j) in enumerate(PAIRS):
        a[i * TILE:(i + 1) * TILE, j * TILE:(j + 1) * TILE] = gram_ref[q] * (1.0 / M)

    for k in range(NT):
        k0, k1 = k * TILE, (k + 1) * TILE
        s[...] = a[k0:k1, k0:k1]
        tile_inverse(s, vt, w.at[k0:k1, k0:k1])
        wk = w[k0:k1, k0:k1]
        if k < NT - 1:
            panel = mul(a[k1:, k0:k1], wk, ((1,), (1,)))
            for j in range(k + 1, NT):
                j0, j1 = j * TILE, (j + 1) * TILE
                a[j0:, j0:j1] -= mul(panel[j0 - k1:], panel[j0 - k1:j1 - k1], ((1,), (1,)))
        if k > 0:
            w[k0:k1, 0:k0] = mul(wk, v[k0:k1, 0:k0], ((1,), (0,)))
        if k < NT - 1:
            v[k1:, k0:k1] = -mul(panel, wk, ((1,), (0,)))
            if k > 0:
                v[k1:, 0:k0] -= mul(panel, w[k0:k1, 0:k0], ((1,), (0,)))
        out_ref[:, k0:k1] = mul(image_ref[:, 0:k1], w[k0:k1, 0:k1], ((1,), (1,)))


def per_device(factor, scales, basis_block):
    f32, bf16, sem = jnp.float32, jnp.bfloat16, pltpu.SemaphoreType.DMA
    vmem = pl.BlockSpec(memory_space=pltpu.VMEM)
    image, gram = pl.pallas_call(
        gather_kernel,
        out_shape=(
            jax.ShapeDtypeStruct((ROWS, COLS), f32),
            jax.ShapeDtypeStruct((len(PAIRS), TILE, TILE), f32),
        ),
        in_specs=[
            pl.BlockSpec(memory_space=pl.ANY),
            pl.BlockSpec(memory_space=pltpu.SMEM),
            pl.BlockSpec(memory_space=pl.ANY),
        ],
        out_specs=(vmem, vmem),
        scratch_shapes=[
            pltpu.VMEM((ROWS, COLS), bf16),
            pltpu.VMEM((ROWS, COLS), bf16),
            pltpu.VMEM((NY, NX, HALF, COLS), bf16),
            pltpu.VMEM((NX, NY, HALF, COLS), bf16),
            pltpu.VMEM((NZ, 2, 2, HALF, COLS), bf16),
            pltpu.VMEM((ROWS, COLS), f32),
            pltpu.VMEM((ROWS, COLS), f32),
            pltpu.VMEM((2, 4, 4, PER_CORE, PIECE, TILE), f32),
            pltpu.VMEM((4, 4, PER_CORE, PIECE, TILE), f32),
            pltpu.VMEM((4, 4, PER_CORE, PIECE, TILE), f32),
            pltpu.VMEM((4, 4, PER_CORE, PIECE, TILE), f32),
            pltpu.VMEM((4, PER_CORE, PIECE, TILE), f32),
            pltpu.VMEM((PER_CORE, PIECE, TILE), f32),
            pltpu.VMEM((2, 4, 4, PER_CORE, PIECE, TILE), f32),
            sem((5,)), sem((6,)), sem((6,)),
            sem((4, 2)), sem((4, 2)), sem((4, 2)), sem((4, 2)),
            sem((2, 9, 2)), sem((2, 9, 2)), sem((2, 9, 2)), sem((2, 9, 2)),
            sem((1,)), sem((1,)),
            sem((7,)), sem((7,)), sem((7,)), sem((7,)),
            sem((4,)), sem((4,)),
        ],
        compiler_params=pltpu.CompilerParams(
            collective_id=0, has_side_effects=True, vmem_limit_bytes=48 * 2**20
        ),
        name="gather_gram",
    )(factor, scales, basis_block)
    tile = pltpu.VMEM((TILE, TILE), f32)
    square = pltpu.VMEM((COLS, COLS), f32)
    return pl.pallas_call(
        refresh_kernel,
        out_shape=jax.ShapeDtypeStruct((ROWS, COLS), f32),
        in_specs=[vmem, vmem],
        out_specs=vmem,
        scratch_shapes=[square, square, square, tile, tile],
        compiler_params=pltpu.CompilerParams(vmem_limit_bytes=32 * 2**20),
        name="refresh",
    )(gram, image)


def solution(mesh):
    return jax.shard_map(
        per_device,
        mesh=mesh,
        in_specs=(P("grp", "blk"), P("grp", "blk"), P("grp", "blk")),
        out_specs=P("grp", "blk"),
        check_vma=False,
    )
```

```python
import jax
import jax.numpy as jnp
from jax import lax
from jax.experimental import pallas as pl
from jax.experimental.pallas import tpu as pltpu
from jax.sharding import PartitionSpec as P

M = 8192
NY, NX, NZ = 4, 4, 16
ROWS, COLS = 256, 512
HALF = ROWS // 2
TILE = 128
NT = COLS // TILE
PAIRS = [(i, j) for i in range(NT) for j in range(i + 1)]
PER_CORE = len(PAIRS) // 2
PIECE = TILE // NZ
SETS = ((0, 3), (3, 2))
SUB = 64
STEP = 8
HIGHEST = lax.Precision.HIGHEST


def place():
    blk, grp = lax.axis_index("blk"), lax.axis_index("grp")
    core, x_hi, y = lax.rem(blk, 2), lax.rem(lax.div(blk, 2), 2), lax.div(blk, 4)
    z, x_lo = lax.div(grp, 2), lax.rem(grp, 2)
    return y, x_hi, x_lo, z, core


def device(y, x, z, core):
    return {"blk": (y * 2 + lax.div(x, 2)) * 2 + core, "grp": z * 2 + lax.rem(x, 2)}


def remote(src, dst, send, recv, to):
    return pltpu.make_async_remote_copy(
        src_ref=src, dst_ref=dst, send_sem=send, recv_sem=recv,
        device_id=to, device_id_type=pl.DeviceIdType.MESH,
    )


def gather_kernel(
    f_ref, scale_ref, b_ref, image_ref, gram_ref,
    f_in, dequant, d_xy, d_yx, basis, image, image_in, part, other, mine, near, far, summed, total,
    own_sem, swap_s, swap_r, xy_s, xy_r, yx_s, yx_r, ring_s, ring_r, sib_s, sib_r,
    pair_s, pair_r, rs_s, rs_r, ag_s, ag_r, across_s, across_r,
):
    y, x_hi, x_lo, z, core = place()
    x = x_hi * 2 + x_lo
    sibling = device(y, x, z, 1 - core)
    partner_x = x_hi * 2 + core
    partner = device(y, partner_x, z, x_lo)
    moved = x_lo != core
    twin = device(y, x_hi * 2 + 1 - x_lo, z, core)

    def x_peer(d):
        return device(y, lax.rem(x + d, NX), z, core)

    def y_peer(d):
        return device(lax.rem(y + d, NY), x, z, core)

    def z_peer(d):
        return device(y, x, lax.rem(z + d, NZ), core)

    load = pltpu.make_async_copy(f_ref, f_in, own_sem.at[4])
    load.start()
    barrier = pltpu.get_barrier_semaphore()

    def greet(to):
        pl.semaphore_signal(barrier, inc=1, device_id=to, device_id_type=pl.DeviceIdType.MESH)

    greet(sibling)
    for d in range(1, 4):
        greet(x_peer(d))
        greet(y_peer(d))
    for d in (1, 15, 2, 14, 4, 8, 12):
        greet(z_peer(d))

    @pl.when(moved)
    def _():
        greet(partner)

    load.wait()
    for i in range(ROWS // TILE):
        for j in range(NT):
            at = (slice(i * TILE, (i + 1) * TILE), slice(j * TILE, (j + 1) * TILE))
            dequant[at] = (f_in[at].astype(jnp.float32) * scale_ref[i, j]).astype(jnp.bfloat16)

    @pl.when(moved)
    def _():
        pl.semaphore_wait(barrier, 15)

    @pl.when(jnp.logical_not(moved))
    def _():
        pl.semaphore_wait(barrier, 14)

    halves = [pl.ds(0, HALF), pl.ds(HALF, HALF)]
    swap_b = [
        remote(b_ref.at[halves[h]], basis.at[z, x_lo, h], swap_s.at[h], swap_r.at[h], partner) for h in range(2)
    ]
    swap_d = [
        remote(dequant.at[halves[0]], d_xy.at[y, partner_x], swap_s.at[2], swap_r.at[2], partner),
        remote(dequant.at[halves[1]], d_yx.at[partner_x, y], swap_s.at[3], swap_r.at[3], partner),
    ]
    kept_b = [pltpu.make_async_copy(b_ref.at[halves[h]], basis.at[z, core, h], own_sem.at[h]) for h in range(2)]
    kept_d = [
        pltpu.make_async_copy(dequant.at[halves[0]], d_xy.at[y, x], own_sem.at[2]),
        pltpu.make_async_copy(dequant.at[halves[1]], d_yx.at[x, y], own_sem.at[3]),
    ]

    @pl.when(moved)
    def _():
        for copy in swap_b:
            copy.start()
        for copy in swap_b:
            copy.wait()
        for copy in swap_d:
            copy.start()

    @pl.when(jnp.logical_not(moved))
    def _():
        for copy in kept_b + kept_d:
            copy.start()
        for copy in kept_b:
            copy.wait()

    ways = [z_peer(1), z_peer(NZ - 1)]

    def origin(way, step):
        return lax.rem(z + (step if way else NZ - step), NZ)

    def hop(way, step, h):
        slot = basis.at[origin(way, step - 1), core, h]
        return remote(slot, slot, ring_s.at[way, step, h], ring_r.at[way, step, h], ways[way])

    def share(way, step, h):
        slot = basis.at[origin(way, step), core, h]
        return remote(slot, slot, sib_s.at[way, step, h], sib_r.at[way, step, h], sibling)

    for h in range(2):
        for way in range(2):
            hop(way, 1, h).start()
    for h in range(2):
        share(0, 0, h).start()

    @pl.when(moved)
    def _():
        for copy in swap_d:
            copy.wait()

    @pl.when(jnp.logical_not(moved))
    def _():
        for copy in kept_d:
            copy.wait()

    def both_ways(refs, send, recv, to):
        return [remote(refs[n], refs[n], send.at[n], recv.at[n], to[n]) for n in (0, 1)]

    x_next, y_next = [x_peer(1), x_peer(NX - 1)], [y_peer(1), y_peer(NY - 1)]
    x_back, x_on = lax.rem(x + NX - 1, NX), lax.rem(x + 1, NX)
    y_back, y_on = lax.rem(y + NY - 1, NY), lax.rem(y + 1, NY)
    quarter = [pl.ds(0, HALF // 2), pl.ds(HALF // 2, HALF // 2)]
    pair = [pl.ds(0, 2), pl.ds(2, 2)]
    first = (
        both_ways([d_xy.at[y, x]] * 2, xy_s.at[0], xy_r.at[0], x_next)
        + both_ways([d_yx.at[x, y]] * 2, yx_s.at[0], yx_r.at[0], y_next)
    )
    first_on = (
        both_ways([d_xy.at[y, x_back, quarter[0]], d_xy.at[y, x_on, quarter[1]]], xy_s.at[1], xy_r.at[1], x_next)
        + both_ways([d_yx.at[x, y_back, quarter[0]], d_yx.at[x, y_on, quarter[1]]], yx_s.at[1], yx_r.at[1], y_next)
    )
    second = (
        both_ways([d_xy.at[y]] * 2, xy_s.at[2], xy_r.at[2], y_next)
        + both_ways([d_yx.at[x]] * 2, yx_s.at[2], yx_r.at[2], x_next)
    )
    second_on = (
        both_ways([d_xy.at[y_back, pair[0]], d_xy.at[y_on, pair[1]]], xy_s.at[3], xy_r.at[3], y_next)
        + both_ways([d_yx.at[x_back, pair[0]], d_yx.at[x_on, pair[1]]], yx_s.at[3], yx_r.at[3], x_next)
    )

    def start(copies):
        for copy in copies:
            copy.start()

    def land(copies):
        for copy in copies:
            copy.wait_recv()

    start(first)

    def relay(step):
        for h in range(2):
            for way in range(2):
                hop(way, step, h).wait_recv()
                hop(way, step + 1, h).start()
                share(way, step, h).start()

    relay(1)
    land(first)
    start(first_on)
    relay(2)
    land(first_on)
    start(second)
    image[...] = jnp.zeros_like(image)
    relay(3)
    relay(4)
    land(second)
    start(second_on)
    relay(5)
    relay(6)
    land(second_on)

    def product(k):
        ky, kx = lax.div(k, NX), lax.rem(k, NX)
        left = jnp.concatenate([d_xy[ky, kx], d_yx[kx, ky]], axis=0)
        right = basis[k].reshape(2 * ROWS, COLS)
        return jnp.dot(left, right, preferred_element_type=jnp.float32)

    def multiply(first, end):
        @pl.loop(first, end)
        def _(step):
            for h in range(2):
                for way in range(2):
                    share(way, step, h).wait_recv()
            image[...] += product(origin(0, step)) + product(origin(1, step))

    for h in range(2):
        share(0, 0, h).wait_recv()
    image[...] += product(z)
    multiply(1, 3)
    for h in range(2):
        for way in range(2):
            hop(way, 7, h).wait_recv()
            if way == h:
                hop(way, 8, h).start()
            share(way, 7, h).start()
    multiply(3, 6)
    for way in range(2):
        hop(way, 8, way).wait_recv()
        share(way, 8, way).start()
    multiply(6, 8)
    for way in range(2):
        share(way, 8, way).wait_recv()
    image[...] += product(origin(0, 8))

    send_image = remote(image, image_in, swap_s.at[4], swap_r.at[4], partner)

    @pl.when(moved)
    def _():
        send_image.start()

    for top in (0, 2):
        width = (top + 2) * TILE
        block = lax.dot_general(
            image[:, top * TILE:width], image[:, 0:width],
            (((0,), (0,)), ((), ())), precision=HIGHEST, preferred_element_type=jnp.float32,
        )
        for q, (i, j) in enumerate(PAIRS):
            if top <= i < top + 2:
                for t in range(NZ):
                    at = (i - top) * TILE + t * PIECE
                    part[q % PER_CORE // 3][q // PER_CORE, t % 4, t // 4, q % PER_CORE % 3] = (
                        block[at:at + PIECE, j * TILE:(j + 1) * TILE]
                    )

    both = range(len(SETS))
    swap = [remote(part[u].at[1 - core], other[u], pair_s.at[u], pair_r.at[u], sibling) for u in both]
    start(swap)
    z_q, z_r = lax.div(z, 4), lax.rem(z, 4)
    offsets = (0, 1, NZ - 1, lax.rem(2 + 12 * core, NZ))
    to_near = [[
        remote(mine[u].at[lax.rem(z_r + offsets[n], 4)], near[u].at[n], rs_s.at[u, n], rs_r.at[u, n], z_peer(offsets[n]))
        for n in (1, 2, 3)
    ] for u in both]
    to_far = [[
        remote(near[u].at[0, lax.rem(z_q + d, 4)], far[u].at[d], rs_s.at[u, 3 + d], rs_r.at[u, 3 + d], z_peer(4 * d))
        for d in (1, 2, 3)
    ] for u in both]
    for u in both:
        swap[u].wait_recv()
        mine[u][...] = part[u][core] + other[u][...]
        start(to_near[u])
    for u in both:
        land(to_near[u])
        near[u][0] = mine[u][z_r] + near[u][1] + near[u][2] + near[u][3]
        start(to_far[u])

    hand = [
        remote(summed[u], total[u].at[core, z_r, z_q], swap_s.at[5 + u], swap_r.at[5 + u], partner) for u in both
    ]
    for u in both:
        land(to_far[u])
        summed[u][...] = near[u][0, z_q] + far[u][1] + far[u][2] + far[u][3]

        @pl.when(moved)
        def _(u=u):
            hand[u].start()

        @pl.when(jnp.logical_not(moved))
        def _(u=u):
            total[u][core, z_r, z_q] = summed[u][...]

    def same(ref, send, recv, to):
        return remote(ref, ref, send, recv, to)

    spread_far = [[
        same(total[u].at[x_lo, z_r, z_q], ag_s.at[u, d], ag_r.at[u, d], z_peer(4 * d)) for d in (1, 2, 3)
    ] for u in both]
    spread_near = [[
        same(total[u].at[x_lo, z_r], ag_s.at[u, 3 + n], ag_r.at[u, 3 + n], z_peer(offsets[n])) for n in (1, 2, 3)
    ] for u in both]
    crossing = [[
        same(total[u].at[x_lo, lax.rem(z_r + NZ - offsets[n], 4)], across_s.at[u, n], across_r.at[u, n], twin)
        for n in range(4)
    ] for u in both]
    for u in both:
        @pl.when(moved)
        def _(u=u):
            hand[u].wait_recv()

        start(spread_far[u])
    for u in both:
        land(spread_far[u])
        start(spread_near[u])
        crossing[u][0].start()
    for u in both:
        for n in (1, 2, 3):
            spread_near[u][n - 1].wait_recv()
            crossing[u][n].start()

    for copy in first + first_on + second + second_on:
        copy.wait_send()
    for h in range(2):
        share(0, 0, h).wait_send()

    @pl.loop(1, 8)
    def _(step):
        for h in range(2):
            for way in range(2):
                hop(way, step, h).wait_send()
                share(way, step, h).wait_send()

    for way in range(2):
        hop(way, 8, way).wait_send()
        share(way, 8, way).wait_send()
    for copy in swap + sum(to_near + to_far + spread_far + spread_near, []):
        copy.wait_send()

    @pl.when(moved)
    def _():
        for copy in hand:
            copy.wait_send()
        send_image.wait()
        image_ref[...] = image_in[...]

    @pl.when(jnp.logical_not(moved))
    def _():
        image_ref[...] = image[...]

    for copy in sum(crossing, []):
        copy.wait()
    for q in range(len(PAIRS)):
        for t in range(NZ):
            piece = total[q % PER_CORE // 3][q // PER_CORE, t % 4, t // 4, q % PER_CORE % 3]
            gram_ref[q, t * PIECE:(t + 1) * PIECE, :] = piece


def tile_inverse(s_ref, v_ref, w_ref):
    vreg = (8, TILE)
    groups = SUB // 8
    row = lax.broadcasted_iota(jnp.int32, vreg, 0)
    eye = lax.broadcasted_iota(jnp.int32, (TILE, TILE), 0) == lax.broadcasted_iota(jnp.int32, (TILE, TILE), 1)
    v_ref[...] = eye.astype(jnp.float32)
    spread = lambda value: jnp.broadcast_to(value, vreg)
    for base in range(0, TILE, SUB):
        strip = [s_ref[base + 8 * g:base + 8 * g + 8, :] for g in range(groups)]
        acts = [v_ref[base + 8 * g:base + 8 * g + 8, :] for g in range(groups)]
        pivots = [jnp.ones(vreg, jnp.float32) for _ in range(groups)]
        for first in range(0, SUB, STEP):
            g0, r0, c0 = first // 8, first % 8, base + first
            live = range(g0, groups)
            srows = [spread(strip[g0][r0 + q:r0 + q + 1, :]) for q in range(STEP)]
            arows = [spread(acts[g0][r0 + q:r0 + q + 1, :]) for q in range(STEP)]
            cols = [{g: spread(strip[g][:, c0 + q:c0 + q + 1]) for g in live} for q in range(STEP)]
            block = {
                (q, r): spread(srows[q][:, c0 + r:c0 + r + 1]) for q in range(STEP) for r in range(q, STEP)
            }
            for q in range(STEP):
                if q % 2 == 0:
                    det = block[q, q] * block[q + 1, q + 1] - block[q, q + 1] * block[q, q + 1]
                    inv = 1.0 / block[q, q]
                    inv_next, pivot_next = block[q, q] * (1.0 / det), det * inv
                else:
                    inv, block[q, q] = inv_next, pivot_next
                pivots[g0] = jnp.where(row == r0 + q, block[q, q], pivots[g0])
                factor = {r: block[q, r] * inv for r in range(q + 1, STEP)}
                for r in range(q + 1, STEP):
                    for t in range(r, STEP):
                        block[r, t] = block[r, t] - factor[r] * block[q, t]
                for g in live:
                    mult = cols[q][g] * inv
                    for r in range(q + 1, STEP):
                        cols[r][g] = cols[r][g] - mult * block[q, r]
                    if g == g0:
                        mult = jnp.where(row > r0 + q, mult, 0.0)
                    strip[g] = strip[g] - mult * srows[q]
                    acts[g] = acts[g] - mult * arows[q]
                for r in range(q + 1, STEP):
                    srows[r] = srows[r] - factor[r] * srows[q]
                    arows[r] = arows[r] - factor[r] * arows[q]
        size = [1.0 / jnp.sqrt(p) for p in pivots]
        upper = jnp.concatenate([s * n for s, n in zip(strip, size)], axis=0)
        done = jnp.concatenate([s * n for s, n in zip(acts, size)], axis=0)
        w_ref[base:base + SUB, :] = done
        below = base + SUB
        if below < TILE:
            s_ref[below:, :] -= mul(upper[:, below:], upper, ((0,), (0,)))
            v_ref[below:, :] -= mul(upper[:, below:], done, ((0,), (0,)))


def mul(a, b, over):
    return lax.dot_general(a, b, (over, ((), ())), precision=HIGHEST, preferred_element_type=jnp.float32)


def refresh_kernel(gram_ref, image_ref, out_ref, a, w, v, s, vt, scaled):
    eye = lax.broadcasted_iota(jnp.int32, (TILE, TILE), 0) == lax.broadcasted_iota(jnp.int32, (TILE, TILE), 1)
    down, along = [], []
    for i in range(NT):
        diagonal = jnp.where(eye, gram_ref[PAIRS.index((i, i))] * (1.0 / M), 0.0)
        down.append(1.0 / jnp.sqrt(jnp.sum(diagonal, axis=1, keepdims=True)))
        along.append(1.0 / jnp.sqrt(jnp.sum(diagonal, axis=0, keepdims=True)))
    for q, (i, j) in enumerate(PAIRS):
        a[i * TILE:(i + 1) * TILE, j * TILE:(j + 1) * TILE] = gram_ref[q] * (1.0 / M) * down[i] * along[j]
    for i in range(NT):
        scaled[:, i * TILE:(i + 1) * TILE] = image_ref[:, i * TILE:(i + 1) * TILE] * along[i]

    for k in range(NT):
        k0, k1 = k * TILE, (k + 1) * TILE
        s[...] = a[k0:k1, k0:k1]
        tile_inverse(s, vt, w.at[k0:k1, k0:k1])
        wk = w[k0:k1, k0:k1]
        if k < NT - 1:
            panel = mul(a[k1:, k0:k1], wk, ((1,), (1,)))
            for j in range(k + 1, NT):
                j0, j1 = j * TILE, (j + 1) * TILE
                a[j0:, j0:j1] -= mul(panel[j0 - k1:], panel[j0 - k1:j1 - k1], ((1,), (1,)))
        if k > 0:
            w[k0:k1, 0:k0] = mul(wk, v[k0:k1, 0:k0], ((1,), (0,)))
        if k < NT - 1:
            v[k1:, k0:k1] = -mul(panel, wk, ((1,), (0,)))
            if k > 0:
                v[k1:, 0:k0] -= mul(panel, w[k0:k1, 0:k0], ((1,), (0,)))
        out_ref[:, k0:k1] = mul(scaled[:, 0:k1], w[k0:k1, 0:k1], ((1,), (1,)))


def per_device(factor, scales, basis_block):
    f32, bf16, sem = jnp.float32, jnp.bfloat16, pltpu.SemaphoreType.DMA
    vmem = pl.BlockSpec(memory_space=pltpu.VMEM)
    image, gram = pl.pallas_call(
        gather_kernel,
        out_shape=(
            jax.ShapeDtypeStruct((ROWS, COLS), f32),
            jax.ShapeDtypeStruct((len(PAIRS), TILE, TILE), f32),
        ),
        in_specs=[
            pl.BlockSpec(memory_space=pltpu.HBM),
            pl.BlockSpec(memory_space=pltpu.SMEM),
            pl.BlockSpec(memory_space=pltpu.HBM),
        ],
        out_specs=(vmem, vmem),
        scratch_shapes=[
            pltpu.VMEM((ROWS, COLS), bf16),
            pltpu.VMEM((ROWS, COLS), bf16),
            pltpu.VMEM((NY, NX, HALF, COLS), bf16),
            pltpu.VMEM((NX, NY, HALF, COLS), bf16),
            pltpu.VMEM((NZ, 2, 2, HALF, COLS), bf16),
            pltpu.VMEM((ROWS, COLS), f32),
            pltpu.VMEM((ROWS, COLS), f32),
            *[
                [pltpu.VMEM((*lead, n, PIECE, TILE), f32) for _, n in SETS]
                for lead in ((2, 4, 4), (4, 4), (4, 4), (4, 4), (4,), (), (2, 4, 4))
            ],
            sem((5,)), sem((7,)), sem((7,)),
            sem((4, 2)), sem((4, 2)), sem((4, 2)), sem((4, 2)),
            sem((2, 9, 2)), sem((2, 9, 2)), sem((2, 9, 2)), sem((2, 9, 2)),
            sem((2,)), sem((2,)),
            sem((2, 7)), sem((2, 7)), sem((2, 7)), sem((2, 7)),
            sem((2, 4)), sem((2, 4)),
        ],
        compiler_params=pltpu.CompilerParams(
            collective_id=0, has_side_effects=True, vmem_limit_bytes=48 * 2**20
        ),
        name="gather_gram",
    )(factor, scales, basis_block)
    tile = pltpu.VMEM((TILE, TILE), f32)
    square = pltpu.VMEM((COLS, COLS), f32)
    return pl.pallas_call(
        refresh_kernel,
        out_shape=jax.ShapeDtypeStruct((ROWS, COLS), f32),
        in_specs=[vmem, vmem],
        out_specs=vmem,
        scratch_shapes=[square, square, square, tile, tile, pltpu.VMEM((ROWS, COLS), f32)],
        compiler_params=pltpu.CompilerParams(vmem_limit_bytes=32 * 2**20),
        name="refresh",
    )(gram, image)


def solution(mesh):
    return jax.shard_map(
        per_device,
        mesh=mesh,
        in_specs=(P("grp", "blk"), P("grp", "blk"), P("grp", "blk")),
        out_specs=P("grp", "blk"),
        check_vma=False,
    )
```

```python
import jax
import jax.numpy as jnp
from jax import lax
from jax.experimental import pallas as pl
from jax.experimental.pallas import tpu as pltpu
from jax.sharding import PartitionSpec as P

M = 8192
NY, NX, NZ = 4, 4, 16
ROWS, COLS = 256, 512
HALF = ROWS // 2
TILE = 128
NT = COLS // TILE
PAIRS = [(i, j) for i in range(NT) for j in range(i + 1)]
PER_CORE = len(PAIRS) // 2
PIECE = TILE // NZ
SETS = ((0, 3), (3, 2))
SUB = 64
STEP = 8
HIGHEST = lax.Precision.HIGHEST


def place():
    blk, grp = lax.axis_index("blk"), lax.axis_index("grp")
    core, x_hi, y = lax.rem(blk, 2), lax.rem(lax.div(blk, 2), 2), lax.div(blk, 4)
    z, x_lo = lax.div(grp, 2), lax.rem(grp, 2)
    return y, x_hi, x_lo, z, core


def device(y, x, z, core):
    return {"blk": (y * 2 + lax.div(x, 2)) * 2 + core, "grp": z * 2 + lax.rem(x, 2)}


def remote(src, dst, send, recv, to):
    return pltpu.make_async_remote_copy(
        src_ref=src, dst_ref=dst, send_sem=send, recv_sem=recv,
        device_id=to, device_id_type=pl.DeviceIdType.MESH,
    )


def gather_kernel(
    f_ref, scale_ref, b_ref, image_ref, gram_ref,
    f_in, dequant, d_xy, d_yx, basis, image, image_in, part, other, mine, near, far, total,
    own_sem, swap_s, swap_r, xy_s, xy_r, yx_s, yx_r, ring_s, ring_r, sib_s, sib_r,
    pair_s, pair_r, rs_s, rs_r, ag_s, ag_r, across_s, across_r,
):
    y, x_hi, x_lo, z, core = place()
    x = x_hi * 2 + x_lo
    sibling = device(y, x, z, 1 - core)
    partner_x = x_hi * 2 + core
    partner = device(y, partner_x, z, x_lo)
    moved = x_lo != core
    twin = device(y, x_hi * 2 + 1 - x_lo, z, core)

    def x_peer(d):
        return device(y, lax.rem(x + d, NX), z, core)

    def y_peer(d):
        return device(lax.rem(y + d, NY), x, z, core)

    def z_peer(d):
        return device(y, x, lax.rem(z + d, NZ), core)

    def owner(d):
        return device(y, partner_x, lax.rem(z + d, NZ), x_lo)

    load = pltpu.make_async_copy(f_ref, f_in, own_sem.at[4])
    load.start()
    barrier = pltpu.get_barrier_semaphore()

    def greet(to):
        pl.semaphore_signal(barrier, inc=1, device_id=to, device_id_type=pl.DeviceIdType.MESH)

    greet(sibling)
    for d in range(1, 4):
        greet(x_peer(d))
        greet(y_peer(d))
    for d in (1, 15, 2, 14, 4, 8, 12):
        greet(z_peer(d))

    @pl.when(moved)
    def _():
        for d in (0, 4, 8, 12):
            greet(owner(d))

    load.wait()
    for i in range(ROWS // TILE):
        for j in range(NT):
            at = (slice(i * TILE, (i + 1) * TILE), slice(j * TILE, (j + 1) * TILE))
            dequant[at] = (f_in[at].astype(jnp.float32) * scale_ref[i, j]).astype(jnp.bfloat16)

    @pl.when(moved)
    def _():
        pl.semaphore_wait(barrier, 18)

    @pl.when(jnp.logical_not(moved))
    def _():
        pl.semaphore_wait(barrier, 14)

    halves = [pl.ds(0, HALF), pl.ds(HALF, HALF)]
    swap_b = [
        remote(b_ref.at[halves[h]], basis.at[z, x_lo, h], swap_s.at[h], swap_r.at[h], partner) for h in range(2)
    ]
    swap_d = [
        remote(dequant.at[halves[0]], d_xy.at[y, partner_x], swap_s.at[2], swap_r.at[2], partner),
        remote(dequant.at[halves[1]], d_yx.at[partner_x, y], swap_s.at[3], swap_r.at[3], partner),
    ]
    kept_b = [pltpu.make_async_copy(b_ref.at[halves[h]], basis.at[z, core, h], own_sem.at[h]) for h in range(2)]
    kept_d = [
        pltpu.make_async_copy(dequant.at[halves[0]], d_xy.at[y, x], own_sem.at[2]),
        pltpu.make_async_copy(dequant.at[halves[1]], d_yx.at[x, y], own_sem.at[3]),
    ]

    @pl.when(moved)
    def _():
        for copy in swap_b:
            copy.start()
        for copy in swap_b:
            copy.wait()
        for copy in swap_d:
            copy.start()

    @pl.when(jnp.logical_not(moved))
    def _():
        for copy in kept_b + kept_d:
            copy.start()
        for copy in kept_b:
            copy.wait()

    ways = [z_peer(1), z_peer(NZ - 1)]

    def origin(way, step):
        return lax.rem(z + (step if way else NZ - step), NZ)

    def hop(way, step, h):
        slot = basis.at[origin(way, step - 1), core, h]
        return remote(slot, slot, ring_s.at[way, step, h], ring_r.at[way, step, h], ways[way])

    def share(way, step, h):
        slot = basis.at[origin(way, step), core, h]
        return remote(slot, slot, sib_s.at[way, step, h], sib_r.at[way, step, h], sibling)

    for h in range(2):
        for way in range(2):
            hop(way, 1, h).start()
    for h in range(2):
        share(0, 0, h).start()

    @pl.when(moved)
    def _():
        for copy in swap_d:
            copy.wait()

    @pl.when(jnp.logical_not(moved))
    def _():
        for copy in kept_d:
            copy.wait()

    def both_ways(refs, send, recv, to):
        return [remote(refs[n], refs[n], send.at[n], recv.at[n], to[n]) for n in (0, 1)]

    x_next, y_next = [x_peer(1), x_peer(NX - 1)], [y_peer(1), y_peer(NY - 1)]
    x_back, x_on = lax.rem(x + NX - 1, NX), lax.rem(x + 1, NX)
    y_back, y_on = lax.rem(y + NY - 1, NY), lax.rem(y + 1, NY)
    quarter = [pl.ds(0, HALF // 2), pl.ds(HALF // 2, HALF // 2)]
    pair = [pl.ds(0, 2), pl.ds(2, 2)]
    first = (
        both_ways([d_xy.at[y, x]] * 2, xy_s.at[0], xy_r.at[0], x_next)
        + both_ways([d_yx.at[x, y]] * 2, yx_s.at[0], yx_r.at[0], y_next)
    )
    first_on = (
        both_ways([d_xy.at[y, x_back, quarter[0]], d_xy.at[y, x_on, quarter[1]]], xy_s.at[1], xy_r.at[1], x_next)
        + both_ways([d_yx.at[x, y_back, quarter[0]], d_yx.at[x, y_on, quarter[1]]], yx_s.at[1], yx_r.at[1], y_next)
    )
    second = (
        both_ways([d_xy.at[y]] * 2, xy_s.at[2], xy_r.at[2], y_next)
        + both_ways([d_yx.at[x]] * 2, yx_s.at[2], yx_r.at[2], x_next)
    )
    second_on = (
        both_ways([d_xy.at[y_back, pair[0]], d_xy.at[y_on, pair[1]]], xy_s.at[3], xy_r.at[3], y_next)
        + both_ways([d_yx.at[x_back, pair[0]], d_yx.at[x_on, pair[1]]], yx_s.at[3], yx_r.at[3], x_next)
    )

    def start(copies):
        for copy in copies:
            copy.start()

    def land(copies):
        for copy in copies:
            copy.wait_recv()

    start(first)

    def relay(step):
        for h in range(2):
            for way in range(2):
                hop(way, step, h).wait_recv()
                hop(way, step + 1, h).start()
                share(way, step, h).start()

    relay(1)
    land(first)
    start(first_on)
    relay(2)
    land(first_on)
    start(second)
    image[...] = jnp.zeros_like(image)
    relay(3)
    relay(4)
    land(second)
    start(second_on)
    relay(5)
    relay(6)
    land(second_on)

    def product(k):
        ky, kx = lax.div(k, NX), lax.rem(k, NX)
        left = jnp.concatenate([d_xy[ky, kx], d_yx[kx, ky]], axis=0)
        right = basis[k].reshape(2 * ROWS, COLS)
        return jnp.dot(left, right, preferred_element_type=jnp.float32)

    def multiply(first, end):
        @pl.loop(first, end)
        def _(step):
            for h in range(2):
                for way in range(2):
                    share(way, step, h).wait_recv()
            image[...] += product(origin(0, step)) + product(origin(1, step))

    for h in range(2):
        share(0, 0, h).wait_recv()
    image[...] += product(z)
    multiply(1, 3)
    for h in range(2):
        for way in range(2):
            hop(way, 7, h).wait_recv()
            if way == h:
                hop(way, 8, h).start()
            share(way, 7, h).start()
    multiply(3, 6)
    for way in range(2):
        hop(way, 8, way).wait_recv()
        share(way, 8, way).start()
    multiply(6, 8)
    for way in range(2):
        share(way, 8, way).wait_recv()
    image[...] += product(origin(0, 8))

    send_image = remote(image, image_in, swap_s.at[4], swap_r.at[4], partner)

    @pl.when(moved)
    def _():
        send_image.start()

    for top in (0, 2):
        width = (top + 2) * TILE
        block = lax.dot_general(
            image[:, top * TILE:width], image[:, 0:width],
            (((0,), (0,)), ((), ())), precision=HIGHEST, preferred_element_type=jnp.float32,
        )
        for q, (i, j) in enumerate(PAIRS):
            if top <= i < top + 2:
                for t in range(NZ):
                    at = (i - top) * TILE + t * PIECE
                    part[q % PER_CORE // 3][q // PER_CORE, t % 4, t // 4, q % PER_CORE % 3] = (
                        block[at:at + PIECE, j * TILE:(j + 1) * TILE]
                    )

    both = range(len(SETS))
    swap = [remote(part[u].at[1 - core], other[u], pair_s.at[u], pair_r.at[u], sibling) for u in both]
    start(swap)
    z_q, z_r = lax.div(z, 4), lax.rem(z, 4)
    offsets = (0, 1, NZ - 1, lax.rem(2 + 12 * core, NZ))
    to_near = [[
        remote(mine[u].at[lax.rem(z_r + offsets[n], 4)], near[u].at[n], rs_s.at[u, n], rs_r.at[u, n], z_peer(offsets[n]))
        for n in (1, 2, 3)
    ] for u in both]
    to_far = [[
        remote(near[u].at[0, lax.rem(z_q + d, 4)], far[u].at[d], rs_s.at[u, 3 + d], rs_r.at[u, 3 + d], owner(4 * d))
        for d in (1, 2, 3)
    ] for u in both]
    for u in both:
        swap[u].wait_recv()
        mine[u][...] = part[u][core] + other[u][...]
        start(to_near[u])
    hand = [
        remote(near[u].at[0, z_q], far[u].at[0], swap_s.at[5 + u], swap_r.at[5 + u], partner) for u in both
    ]
    for u in both:
        land(to_near[u])
        near[u][0] = mine[u][z_r] + near[u][1] + near[u][2] + near[u][3]
        start(to_far[u])

        @pl.when(moved)
        def _(u=u):
            hand[u].start()

        @pl.when(jnp.logical_not(moved))
        def _(u=u):
            far[u][0] = near[u][0, z_q]

    def same(ref, send, recv, to):
        return remote(ref, ref, send, recv, to)

    spread_far = [[
        same(total[u].at[x_lo, z_r, z_q], ag_s.at[u, d], ag_r.at[u, d], z_peer(4 * d)) for d in (1, 2, 3)
    ] for u in both]
    spread_near = [[
        same(total[u].at[x_lo, z_r], ag_s.at[u, 3 + n], ag_r.at[u, 3 + n], z_peer(offsets[n])) for n in (1, 2, 3)
    ] for u in both]
    crossing = [[
        same(total[u].at[x_lo, lax.rem(z_r + NZ - offsets[n], 4)], across_s.at[u, n], across_r.at[u, n], twin)
        for n in range(4)
    ] for u in both]
    for u in both:
        land(to_far[u])

        @pl.when(moved)
        def _(u=u):
            hand[u].wait_recv()

        total[u][x_lo, z_r, z_q] = far[u][0] + far[u][1] + far[u][2] + far[u][3]
        start(spread_far[u])
    for u in both:
        land(spread_far[u])
        start(spread_near[u])
        crossing[u][0].start()
    for u in both:
        for n in (1, 2, 3):
            spread_near[u][n - 1].wait_recv()
            crossing[u][n].start()

    for copy in first + first_on + second + second_on:
        copy.wait_send()
    for h in range(2):
        share(0, 0, h).wait_send()

    @pl.loop(1, 8)
    def _(step):
        for h in range(2):
            for way in range(2):
                hop(way, step, h).wait_send()
                share(way, step, h).wait_send()

    for way in range(2):
        hop(way, 8, way).wait_send()
        share(way, 8, way).wait_send()
    for copy in swap + sum(to_near + to_far + spread_far + spread_near, []):
        copy.wait_send()

    @pl.when(moved)
    def _():
        for copy in hand:
            copy.wait_send()
        send_image.wait()
        image_ref[...] = image_in[...]

    @pl.when(jnp.logical_not(moved))
    def _():
        image_ref[...] = image[...]

    for copy in sum(crossing, []):
        copy.wait()
    for q in range(len(PAIRS)):
        for t in range(NZ):
            piece = total[q % PER_CORE // 3][q // PER_CORE, t % 4, t // 4, q % PER_CORE % 3]
            gram_ref[q, t * PIECE:(t + 1) * PIECE, :] = piece


def reciprocal(value):
    guess = pl.reciprocal(value, approx=True)
    guess = guess * (2.0 - value * guess)
    return guess * (2.0 - value * guess)


def tile_inverse(s_ref, v_ref, w_ref):
    vreg = (8, TILE)
    groups = SUB // 8
    row = lax.broadcasted_iota(jnp.int32, vreg, 0)
    eye = lax.broadcasted_iota(jnp.int32, (TILE, TILE), 0) == lax.broadcasted_iota(jnp.int32, (TILE, TILE), 1)
    v_ref[...] = eye.astype(jnp.float32)
    spread = lambda value: jnp.broadcast_to(value, vreg)
    for base in range(0, TILE, SUB):
        strip = [s_ref[base + 8 * g:base + 8 * g + 8, :] for g in range(groups)]
        acts = [v_ref[base + 8 * g:base + 8 * g + 8, :] for g in range(groups)]
        pivots = [jnp.ones(vreg, jnp.float32) for _ in range(groups)]
        for first in range(0, SUB, STEP):
            g0, r0, c0 = first // 8, first % 8, base + first
            live = range(g0, groups)
            srows = [spread(strip[g0][r0 + q:r0 + q + 1, :]) for q in range(STEP)]
            arows = [spread(acts[g0][r0 + q:r0 + q + 1, :]) for q in range(STEP)]
            cols = [{g: spread(strip[g][:, c0 + q:c0 + q + 1]) for g in live} for q in range(STEP)]
            block = {
                (q, r): spread(srows[q][:, c0 + r:c0 + r + 1]) for q in range(STEP) for r in range(q, STEP)
            }
            for q in range(STEP):
                if q % 2 == 0:
                    det = block[q, q] * block[q + 1, q + 1] - block[q, q + 1] * block[q, q + 1]
                    inv = reciprocal(block[q, q])
                    inv_next, pivot_next = block[q, q] * reciprocal(det), det * inv
                else:
                    inv, block[q, q] = inv_next, pivot_next
                pivots[g0] = jnp.where(row == r0 + q, block[q, q], pivots[g0])
                factor = {r: block[q, r] * inv for r in range(q + 1, STEP)}
                for r in range(q + 1, STEP):
                    for t in range(r, STEP):
                        block[r, t] = block[r, t] - factor[r] * block[q, t]
                for g in live:
                    mult = cols[q][g] * inv
                    for r in range(q + 1, STEP):
                        cols[r][g] = cols[r][g] - mult * block[q, r]
                    if g == g0:
                        mult = jnp.where(row > r0 + q, mult, 0.0)
                    strip[g] = strip[g] - mult * srows[q]
                    acts[g] = acts[g] - mult * arows[q]
                for r in range(q + 1, STEP):
                    srows[r] = srows[r] - factor[r] * srows[q]
                    arows[r] = arows[r] - factor[r] * arows[q]
        size = [1.0 / jnp.sqrt(p) for p in pivots]
        upper = jnp.concatenate([s * n for s, n in zip(strip, size)], axis=0)
        done = jnp.concatenate([s * n for s, n in zip(acts, size)], axis=0)
        w_ref[base:base + SUB, :] = done
        below = base + SUB
        if below < TILE:
            s_ref[below:, :] -= mul(upper[:, below:], upper, ((0,), (0,)))
            v_ref[below:, :] -= mul(upper[:, below:], done, ((0,), (0,)))


def mul(a, b, over):
    return lax.dot_general(a, b, (over, ((), ())), precision=HIGHEST, preferred_element_type=jnp.float32)


def refresh_kernel(gram_ref, image_ref, out_ref, a, w, v, s, vt, scaled):
    eye = lax.broadcasted_iota(jnp.int32, (TILE, TILE), 0) == lax.broadcasted_iota(jnp.int32, (TILE, TILE), 1)
    down, along = [], []
    for i in range(NT):
        diagonal = jnp.where(eye, gram_ref[PAIRS.index((i, i))] * (1.0 / M), 0.0)
        down.append(1.0 / jnp.sqrt(jnp.sum(diagonal, axis=1, keepdims=True)))
        along.append(1.0 / jnp.sqrt(jnp.sum(diagonal, axis=0, keepdims=True)))
    for q, (i, j) in enumerate(PAIRS):
        a[i * TILE:(i + 1) * TILE, j * TILE:(j + 1) * TILE] = gram_ref[q] * (1.0 / M) * down[i] * along[j]
    for i in range(NT):
        scaled[:, i * TILE:(i + 1) * TILE] = image_ref[:, i * TILE:(i + 1) * TILE] * along[i]

    for k in range(NT):
        k0, k1 = k * TILE, (k + 1) * TILE
        s[...] = a[k0:k1, k0:k1]
        tile_inverse(s, vt, w.at[k0:k1, k0:k1])
        wk = w[k0:k1, k0:k1]
        if k < NT - 1:
            panel = mul(a[k1:, k0:k1], wk, ((1,), (1,)))
            for j in range(k + 1, NT):
                j0, j1 = j * TILE, (j + 1) * TILE
                a[j0:, j0:j1] -= mul(panel[j0 - k1:], panel[j0 - k1:j1 - k1], ((1,), (1,)))
        if k > 0:
            w[k0:k1, 0:k0] = mul(wk, v[k0:k1, 0:k0], ((1,), (0,)))
        if k < NT - 1:
            v[k1:, k0:k1] = -mul(panel, wk, ((1,), (0,)))
            if k > 0:
                v[k1:, 0:k0] -= mul(panel, w[k0:k1, 0:k0], ((1,), (0,)))
        out_ref[:, k0:k1] = mul(scaled[:, 0:k1], w[k0:k1, 0:k1], ((1,), (1,)))


def per_device(factor, scales, basis_block):
    f32, bf16, sem = jnp.float32, jnp.bfloat16, pltpu.SemaphoreType.DMA
    vmem = pl.BlockSpec(memory_space=pltpu.VMEM)
    image, gram = pl.pallas_call(
        gather_kernel,
        out_shape=(
            jax.ShapeDtypeStruct((ROWS, COLS), f32),
            jax.ShapeDtypeStruct((len(PAIRS), TILE, TILE), f32),
        ),
        in_specs=[
            pl.BlockSpec(memory_space=pltpu.HBM),
            pl.BlockSpec(memory_space=pltpu.SMEM),
            pl.BlockSpec(memory_space=pltpu.HBM),
        ],
        out_specs=(vmem, vmem),
        scratch_shapes=[
            pltpu.VMEM((ROWS, COLS), bf16),
            pltpu.VMEM((ROWS, COLS), bf16),
            pltpu.VMEM((NY, NX, HALF, COLS), bf16),
            pltpu.VMEM((NX, NY, HALF, COLS), bf16),
            pltpu.VMEM((NZ, 2, 2, HALF, COLS), bf16),
            pltpu.VMEM((ROWS, COLS), f32),
            pltpu.VMEM((ROWS, COLS), f32),
            *[
                [pltpu.VMEM((*lead, n, PIECE, TILE), f32) for _, n in SETS]
                for lead in ((2, 4, 4), (4, 4), (4, 4), (4, 4), (4,), (2, 4, 4))
            ],
            sem((5,)), sem((7,)), sem((7,)),
            sem((4, 2)), sem((4, 2)), sem((4, 2)), sem((4, 2)),
            sem((2, 9, 2)), sem((2, 9, 2)), sem((2, 9, 2)), sem((2, 9, 2)),
            sem((2,)), sem((2,)),
            sem((2, 7)), sem((2, 7)), sem((2, 7)), sem((2, 7)),
            sem((2, 4)), sem((2, 4)),
        ],
        compiler_params=pltpu.CompilerParams(
            collective_id=0, has_side_effects=True, vmem_limit_bytes=64 * 2**20
        ),
        name="gather_gram",
    )(factor, scales, basis_block)
    tile = pltpu.VMEM((TILE, TILE), f32)
    square = pltpu.VMEM((COLS, COLS), f32)
    return pl.pallas_call(
        refresh_kernel,
        out_shape=jax.ShapeDtypeStruct((ROWS, COLS), f32),
        in_specs=[vmem, vmem],
        out_specs=vmem,
        scratch_shapes=[square, square, square, tile, tile, pltpu.VMEM((ROWS, COLS), f32)],
        compiler_params=pltpu.CompilerParams(vmem_limit_bytes=32 * 2**20),
        name="refresh",
    )(gram, image)


def solution(mesh):
    return jax.shard_map(
        per_device,
        mesh=mesh,
        in_specs=(P("grp", "blk"), P("grp", "blk"), P("grp", "blk")),
        out_specs=P("grp", "blk"),
        check_vma=False,
    )
```

```python
import jax
import jax.numpy as jnp
from jax import lax
from jax.experimental import pallas as pl
from jax.experimental.pallas import tpu as pltpu
from jax.sharding import PartitionSpec as P

M = 8192
NY, NX, NZ = 4, 4, 16
ROWS, COLS = 256, 512
HALF = ROWS // 2
TILE = 128
NT = COLS // TILE
PAIRS = [(i, j) for i in range(NT) for j in range(i + 1)]
PER_CORE = len(PAIRS) // 2
PIECE = TILE // NZ
SETS = ((0, 3), (3, 2))
SUB = 64
STEP = 8
HIGHEST = lax.Precision.HIGHEST


def place():
    blk, grp = lax.axis_index("blk"), lax.axis_index("grp")
    core, x_hi, y = lax.rem(blk, 2), lax.rem(lax.div(blk, 2), 2), lax.div(blk, 4)
    z, x_lo = lax.div(grp, 2), lax.rem(grp, 2)
    return y, x_hi, x_lo, z, core


def device(y, x, z, core):
    return {"blk": (y * 2 + lax.div(x, 2)) * 2 + core, "grp": z * 2 + lax.rem(x, 2)}


def remote(src, dst, send, recv, to):
    return pltpu.make_async_remote_copy(
        src_ref=src, dst_ref=dst, send_sem=send, recv_sem=recv,
        device_id=to, device_id_type=pl.DeviceIdType.MESH,
    )


def gather_kernel(
    f_ref, scale_ref, b_ref, image_ref, gram_ref,
    f_in, dequant, d_xy, d_yx, basis, image, image_in, part, other, mine, near, far, total,
    own_sem, swap_s, swap_r, xy_s, xy_r, yx_s, yx_r, ring_s, ring_r, sib_s, sib_r,
    pair_s, pair_r, rs_s, rs_r, ag_s, ag_r, across_s, across_r,
):
    y, x_hi, x_lo, z, core = place()
    x = x_hi * 2 + x_lo
    sibling = device(y, x, z, 1 - core)
    partner_x = x_hi * 2 + core
    partner = device(y, partner_x, z, x_lo)
    moved = x_lo != core
    twin = device(y, x_hi * 2 + 1 - x_lo, z, core)

    def x_peer(d):
        return device(y, lax.rem(x + d, NX), z, core)

    def y_peer(d):
        return device(lax.rem(y + d, NY), x, z, core)

    def z_peer(d):
        return device(y, x, lax.rem(z + d, NZ), core)

    def owner(d):
        return device(y, partner_x, lax.rem(z + d, NZ), x_lo)

    load = pltpu.make_async_copy(f_ref, f_in, own_sem.at[4])
    load.start()
    barrier = pltpu.get_barrier_semaphore()

    def greet(to):
        pl.semaphore_signal(barrier, inc=1, device_id=to, device_id_type=pl.DeviceIdType.MESH)

    greet(sibling)
    for d in range(1, 4):
        greet(x_peer(d))
        greet(y_peer(d))
    for d in (1, 15, 2, 14, 4, 8, 12):
        greet(z_peer(d))

    @pl.when(moved)
    def _():
        for d in (0, 4, 8, 12):
            greet(owner(d))

    load.wait()
    for i in range(ROWS // TILE):
        for j in range(NT):
            at = (slice(i * TILE, (i + 1) * TILE), slice(j * TILE, (j + 1) * TILE))
            dequant[at] = (f_in[at].astype(jnp.float32) * scale_ref[i, j]).astype(jnp.bfloat16)

    @pl.when(moved)
    def _():
        pl.semaphore_wait(barrier, 18)

    @pl.when(jnp.logical_not(moved))
    def _():
        pl.semaphore_wait(barrier, 14)

    halves = [pl.ds(0, HALF), pl.ds(HALF, HALF)]
    swap_b = [
        remote(b_ref.at[halves[h]], basis.at[z, x_lo, h], swap_s.at[h], swap_r.at[h], partner) for h in range(2)
    ]
    swap_d = [
        remote(dequant.at[halves[0]], d_xy.at[y, partner_x], swap_s.at[2], swap_r.at[2], partner),
        remote(dequant.at[halves[1]], d_yx.at[partner_x, y], swap_s.at[3], swap_r.at[3], partner),
    ]
    kept_b = [pltpu.make_async_copy(b_ref.at[halves[h]], basis.at[z, core, h], own_sem.at[h]) for h in range(2)]
    kept_d = [
        pltpu.make_async_copy(dequant.at[halves[0]], d_xy.at[y, x], own_sem.at[2]),
        pltpu.make_async_copy(dequant.at[halves[1]], d_yx.at[x, y], own_sem.at[3]),
    ]

    @pl.when(moved)
    def _():
        for copy in swap_b:
            copy.start()
        for copy in swap_b:
            copy.wait()
        for copy in swap_d:
            copy.start()

    @pl.when(jnp.logical_not(moved))
    def _():
        for copy in kept_b + kept_d:
            copy.start()
        for copy in kept_b:
            copy.wait()

    ways = [z_peer(1), z_peer(NZ - 1)]

    def origin(way, step):
        return lax.rem(z + (step if way else NZ - step), NZ)

    def hop(way, step, h):
        slot = basis.at[origin(way, step - 1), core, h]
        return remote(slot, slot, ring_s.at[way, step, h], ring_r.at[way, step, h], ways[way])

    def share(way, step, h):
        slot = basis.at[origin(way, step), core, h]
        return remote(slot, slot, sib_s.at[way, step, h], sib_r.at[way, step, h], sibling)

    for h in range(2):
        for way in range(2):
            hop(way, 1, h).start()
    for h in range(2):
        share(0, 0, h).start()

    @pl.when(moved)
    def _():
        for copy in swap_d:
            copy.wait()

    @pl.when(jnp.logical_not(moved))
    def _():
        for copy in kept_d:
            copy.wait()

    def both_ways(refs, send, recv, to):
        return [remote(refs[n], refs[n], send.at[n], recv.at[n], to[n]) for n in (0, 1)]

    x_next, y_next = [x_peer(1), x_peer(NX - 1)], [y_peer(1), y_peer(NY - 1)]
    x_back, x_on = lax.rem(x + NX - 1, NX), lax.rem(x + 1, NX)
    y_back, y_on = lax.rem(y + NY - 1, NY), lax.rem(y + 1, NY)
    quarter = [pl.ds(0, HALF // 2), pl.ds(HALF // 2, HALF // 2)]
    pair = [pl.ds(0, 2), pl.ds(2, 2)]
    first = (
        both_ways([d_xy.at[y, x]] * 2, xy_s.at[0], xy_r.at[0], x_next)
        + both_ways([d_yx.at[x, y]] * 2, yx_s.at[0], yx_r.at[0], y_next)
    )
    first_on = (
        both_ways([d_xy.at[y, x_back, quarter[0]], d_xy.at[y, x_on, quarter[1]]], xy_s.at[1], xy_r.at[1], x_next)
        + both_ways([d_yx.at[x, y_back, quarter[0]], d_yx.at[x, y_on, quarter[1]]], yx_s.at[1], yx_r.at[1], y_next)
    )
    second = (
        both_ways([d_xy.at[y]] * 2, xy_s.at[2], xy_r.at[2], y_next)
        + both_ways([d_yx.at[x]] * 2, yx_s.at[2], yx_r.at[2], x_next)
    )
    second_on = (
        both_ways([d_xy.at[y_back, pair[0]], d_xy.at[y_on, pair[1]]], xy_s.at[3], xy_r.at[3], y_next)
        + both_ways([d_yx.at[x_back, pair[0]], d_yx.at[x_on, pair[1]]], yx_s.at[3], yx_r.at[3], x_next)
    )

    def start(copies):
        for copy in copies:
            copy.start()

    def land(copies):
        for copy in copies:
            copy.wait_recv()

    start(first)

    def relay(step):
        for h in range(2):
            for way in range(2):
                hop(way, step, h).wait_recv()
                hop(way, step + 1, h).start()
                share(way, step, h).start()

    relay(1)
    land(first)
    start(first_on)
    relay(2)
    land(first_on)
    start(second)
    image[...] = jnp.zeros_like(image)
    relay(3)
    relay(4)
    land(second)
    start(second_on)
    relay(5)
    relay(6)
    land(second_on)

    def product(k):
        ky, kx = lax.div(k, NX), lax.rem(k, NX)
        left = jnp.concatenate([d_xy[ky, kx], d_yx[kx, ky]], axis=0)
        right = basis[k].reshape(2 * ROWS, COLS)
        return jnp.dot(left, right, preferred_element_type=jnp.float32)

    def multiply(first, end):
        @pl.loop(first, end)
        def _(step):
            for h in range(2):
                for way in range(2):
                    share(way, step, h).wait_recv()
            image[...] += product(origin(0, step)) + product(origin(1, step))

    for h in range(2):
        share(0, 0, h).wait_recv()
    image[...] += product(z)
    multiply(1, 3)
    for h in range(2):
        for way in range(2):
            hop(way, 7, h).wait_recv()
            if way == h:
                hop(way, 8, h).start()
            share(way, 7, h).start()
    multiply(3, 6)
    for way in range(2):
        hop(way, 8, way).wait_recv()
        share(way, 8, way).start()
    multiply(6, 8)
    for way in range(2):
        share(way, 8, way).wait_recv()
    image[...] += product(origin(0, 8))

    send_image = remote(image, image_in, swap_s.at[4], swap_r.at[4], partner)

    @pl.when(moved)
    def _():
        send_image.start()

    for top in (0, 2):
        width = (top + 2) * TILE
        block = lax.dot_general(
            image[:, top * TILE:width], image[:, 0:width],
            (((0,), (0,)), ((), ())), precision=HIGHEST, preferred_element_type=jnp.float32,
        )
        for q, (i, j) in enumerate(PAIRS):
            if top <= i < top + 2:
                for t in range(NZ):
                    at = (i - top) * TILE + t * PIECE
                    part[q % PER_CORE // 3][q // PER_CORE, t % 4, t // 4, q % PER_CORE % 3] = (
                        block[at:at + PIECE, j * TILE:(j + 1) * TILE]
                    )

    both = range(len(SETS))
    swap = [remote(part[u].at[1 - core], other[u], pair_s.at[u], pair_r.at[u], sibling) for u in both]
    start(swap)
    z_q, z_r = lax.div(z, 4), lax.rem(z, 4)
    offsets = (0, 1, NZ - 1, lax.rem(2 + 12 * core, NZ))
    to_near = [[
        remote(mine[u].at[lax.rem(z_r + offsets[n], 4)], near[u].at[n], rs_s.at[u, n], rs_r.at[u, n], z_peer(offsets[n]))
        for n in (1, 2, 3)
    ] for u in both]
    to_far = [[
        remote(near[u].at[0, lax.rem(z_q + d, 4)], far[u].at[d], rs_s.at[u, 3 + d], rs_r.at[u, 3 + d], owner(4 * d))
        for d in (1, 2, 3)
    ] for u in both]
    for u in both:
        swap[u].wait_recv()
        mine[u][...] = part[u][core] + other[u][...]
        start(to_near[u])
    hand = [
        remote(near[u].at[0, z_q], far[u].at[0], swap_s.at[5 + u], swap_r.at[5 + u], partner) for u in both
    ]
    for u in both:
        land(to_near[u])
        near[u][0] = mine[u][z_r] + near[u][1] + near[u][2] + near[u][3]
        start(to_far[u])

        @pl.when(moved)
        def _(u=u):
            hand[u].start()

        @pl.when(jnp.logical_not(moved))
        def _(u=u):
            far[u][0] = near[u][0, z_q]

    def same(ref, send, recv, to):
        return remote(ref, ref, send, recv, to)

    spread_far = [[
        same(total[u].at[x_lo, z_r, z_q], ag_s.at[u, d], ag_r.at[u, d], z_peer(4 * d)) for d in (1, 2, 3)
    ] for u in both]
    spread_near = [[
        same(total[u].at[x_lo, z_r], ag_s.at[u, 3 + n], ag_r.at[u, 3 + n], z_peer(offsets[n])) for n in (1, 2, 3)
    ] for u in both]
    crossing = [[
        same(total[u].at[x_lo, lax.rem(z_r + NZ - offsets[n], 4)], across_s.at[u, n], across_r.at[u, n], twin)
        for n in range(4)
    ] for u in both]
    for u in both:
        land(to_far[u])

        @pl.when(moved)
        def _(u=u):
            hand[u].wait_recv()

        total[u][x_lo, z_r, z_q] = far[u][0] + far[u][1] + far[u][2] + far[u][3]
        start(spread_far[u])
    for u in both:
        land(spread_far[u])
        start(spread_near[u])
        crossing[u][0].start()
    for u in both:
        for n in (1, 2, 3):
            spread_near[u][n - 1].wait_recv()
            crossing[u][n].start()

    for copy in first + first_on + second + second_on:
        copy.wait_send()
    for h in range(2):
        share(0, 0, h).wait_send()

    @pl.loop(1, 8)
    def _(step):
        for h in range(2):
            for way in range(2):
                hop(way, step, h).wait_send()
                share(way, step, h).wait_send()

    for way in range(2):
        hop(way, 8, way).wait_send()
        share(way, 8, way).wait_send()
    for copy in swap + sum(to_near + to_far + spread_far + spread_near, []):
        copy.wait_send()

    @pl.when(moved)
    def _():
        for copy in hand:
            copy.wait_send()
        send_image.wait()
        image_ref[...] = image_in[...]

    @pl.when(jnp.logical_not(moved))
    def _():
        image_ref[...] = image[...]

    for copy in sum(crossing, []):
        copy.wait()
    for q in range(len(PAIRS)):
        for t in range(NZ):
            piece = total[q % PER_CORE // 3][q // PER_CORE, t % 4, t // 4, q % PER_CORE % 3]
            gram_ref[q, t * PIECE:(t + 1) * PIECE, :] = piece


def tile_inverse(s_ref, v_ref, w_ref):
    vreg = (8, TILE)
    groups = SUB // 8
    row = lax.broadcasted_iota(jnp.int32, vreg, 0)
    eye = lax.broadcasted_iota(jnp.int32, (TILE, TILE), 0) == lax.broadcasted_iota(jnp.int32, (TILE, TILE), 1)
    v_ref[...] = eye.astype(jnp.float32)
    spread = lambda value: jnp.broadcast_to(value, vreg)
    for base in range(0, TILE, SUB):
        strip = [s_ref[base + 8 * g:base + 8 * g + 8, :] for g in range(groups)]
        acts = [v_ref[base + 8 * g:base + 8 * g + 8, :] for g in range(groups)]
        pivots = [jnp.ones(vreg, jnp.float32) for _ in range(groups)]
        for first in range(0, SUB, STEP):
            g0, r0, c0 = first // 8, first % 8, base + first
            live = range(g0, groups)
            srows = [spread(strip[g0][r0 + q:r0 + q + 1, :]) for q in range(STEP)]
            arows = [spread(acts[g0][r0 + q:r0 + q + 1, :]) for q in range(STEP)]
            cols = [{g: spread(strip[g][:, c0 + q:c0 + q + 1]) for g in live} for q in range(STEP)]
            block = {
                (q, r): spread(srows[q][:, c0 + r:c0 + r + 1]) for q in range(STEP) for r in range(q, STEP)
            }
            for q in range(STEP):
                if q % 2 == 0:
                    det = block[q, q] * block[q + 1, q + 1] - block[q, q + 1] * block[q, q + 1]
                    inv = 1.0 / block[q, q]
                    inv_next, pivot_next = block[q, q] * (1.0 / det), det * inv
                else:
                    inv, block[q, q] = inv_next, pivot_next
                pivots[g0] = jnp.where(row == r0 + q, block[q, q], pivots[g0])
                factor = {r: block[q, r] * inv for r in range(q + 1, STEP)}
                for r in range(q + 1, STEP):
                    for t in range(r, STEP):
                        block[r, t] = block[r, t] - factor[r] * block[q, t]
                for g in live:
                    mult = cols[q][g] * inv
                    for r in range(q + 1, STEP):
                        cols[r][g] = cols[r][g] - mult * block[q, r]
                    if g == g0:
                        mult = jnp.where(row > r0 + q, mult, 0.0)
                    strip[g] = strip[g] - mult * srows[q]
                    acts[g] = acts[g] - mult * arows[q]
                for r in range(q + 1, STEP):
                    srows[r] = srows[r] - factor[r] * srows[q]
                    arows[r] = arows[r] - factor[r] * arows[q]
        size = [1.0 / jnp.sqrt(p) for p in pivots]
        upper = jnp.concatenate([s * n for s, n in zip(strip, size)], axis=0)
        done = jnp.concatenate([s * n for s, n in zip(acts, size)], axis=0)
        w_ref[base:base + SUB, :] = done
        below = base + SUB
        if below < TILE:
            s_ref[below:, :] -= mul(upper[:, below:], upper, ((0,), (0,)))
            v_ref[below:, :] -= mul(upper[:, below:], done, ((0,), (0,)))


def mul(a, b, over):
    return lax.dot_general(a, b, (over, ((), ())), precision=HIGHEST, preferred_element_type=jnp.float32)


def refresh_kernel(gram_in, image_in, out_ref, gram_ref, image_ref, a, w, v, s, vt, scaled, load_sem):
    load_gram = pltpu.make_async_copy(gram_in, gram_ref, load_sem.at[0])
    load_image = pltpu.make_async_copy(image_in, image_ref, load_sem.at[1])
    load_gram.start()
    load_image.start()
    load_gram.wait()
    eye = lax.broadcasted_iota(jnp.int32, (TILE, TILE), 0) == lax.broadcasted_iota(jnp.int32, (TILE, TILE), 1)
    down, along = [], []
    for i in range(NT):
        diagonal = jnp.where(eye, gram_ref[PAIRS.index((i, i))] * (1.0 / M), 0.0)
        down.append(1.0 / jnp.sqrt(jnp.sum(diagonal, axis=1, keepdims=True)))
        along.append(1.0 / jnp.sqrt(jnp.sum(diagonal, axis=0, keepdims=True)))
    for q, (i, j) in enumerate(PAIRS):
        a[i * TILE:(i + 1) * TILE, j * TILE:(j + 1) * TILE] = gram_ref[q] * (1.0 / M) * down[i] * along[j]
    load_image.wait()
    for i in range(NT):
        scaled[:, i * TILE:(i + 1) * TILE] = image_ref[:, i * TILE:(i + 1) * TILE] * along[i]

    for k in range(NT):
        k0, k1 = k * TILE, (k + 1) * TILE
        s[...] = a[k0:k1, k0:k1]
        tile_inverse(s, vt, w.at[k0:k1, k0:k1])
        wk = w[k0:k1, k0:k1]
        if k < NT - 1:
            panel = mul(a[k1:, k0:k1], wk, ((1,), (1,)))
            for j in range(k + 1, NT):
                j0, j1 = j * TILE, (j + 1) * TILE
                a[j0:, j0:j1] -= mul(panel[j0 - k1:], panel[j0 - k1:j1 - k1], ((1,), (1,)))
        if k > 0:
            w[k0:k1, 0:k0] = mul(wk, v[k0:k1, 0:k0], ((1,), (0,)))
        if k < NT - 1:
            v[k1:, k0:k1] = -mul(panel, wk, ((1,), (0,)))
            if k > 0:
                v[k1:, 0:k0] -= mul(panel, w[k0:k1, 0:k0], ((1,), (0,)))
        out_ref[:, k0:k1] = mul(scaled[:, 0:k1], w[k0:k1, 0:k1], ((1,), (1,)))


def per_device(factor, scales, basis_block):
    f32, bf16, sem = jnp.float32, jnp.bfloat16, pltpu.SemaphoreType.DMA
    vmem = pl.BlockSpec(memory_space=pltpu.VMEM)
    image, gram = pl.pallas_call(
        gather_kernel,
        out_shape=(
            jax.ShapeDtypeStruct((ROWS, COLS), f32),
            jax.ShapeDtypeStruct((len(PAIRS), TILE, TILE), f32),
        ),
        in_specs=[
            pl.BlockSpec(memory_space=pltpu.HBM),
            pl.BlockSpec(memory_space=pltpu.SMEM),
            pl.BlockSpec(memory_space=pltpu.HBM),
        ],
        out_specs=(vmem, vmem),
        scratch_shapes=[
            pltpu.VMEM((ROWS, COLS), bf16),
            pltpu.VMEM((ROWS, COLS), bf16),
            pltpu.VMEM((NY, NX, HALF, COLS), bf16),
            pltpu.VMEM((NX, NY, HALF, COLS), bf16),
            pltpu.VMEM((NZ, 2, 2, HALF, COLS), bf16),
            pltpu.VMEM((ROWS, COLS), f32),
            pltpu.VMEM((ROWS, COLS), f32),
            *[
                [pltpu.VMEM((*lead, n, PIECE, TILE), f32) for _, n in SETS]
                for lead in ((2, 4, 4), (4, 4), (4, 4), (4, 4), (4,), (2, 4, 4))
            ],
            sem((5,)), sem((7,)), sem((7,)),
            sem((4, 2)), sem((4, 2)), sem((4, 2)), sem((4, 2)),
            sem((2, 9, 2)), sem((2, 9, 2)), sem((2, 9, 2)), sem((2, 9, 2)),
            sem((2,)), sem((2,)),
            sem((2, 7)), sem((2, 7)), sem((2, 7)), sem((2, 7)),
            sem((2, 4)), sem((2, 4)),
        ],
        compiler_params=pltpu.CompilerParams(
            collective_id=0, has_side_effects=True, vmem_limit_bytes=64 * 2**20
        ),
        name="gather_gram",
    )(factor, scales, basis_block)
    tile = pltpu.VMEM((TILE, TILE), f32)
    square = pltpu.VMEM((COLS, COLS), f32)
    return pl.pallas_call(
        refresh_kernel,
        out_shape=jax.ShapeDtypeStruct((ROWS, COLS), f32),
        in_specs=[pl.BlockSpec(memory_space=pltpu.HBM)] * 2,
        out_specs=vmem,
        scratch_shapes=[
            pltpu.VMEM((len(PAIRS), TILE, TILE), f32), pltpu.VMEM((ROWS, COLS), f32),
            square, square, square, tile, tile, pltpu.VMEM((ROWS, COLS), f32), sem((2,)),
        ],
        compiler_params=pltpu.CompilerParams(vmem_limit_bytes=64 * 2**20),
        name="refresh",
    )(gram, image)


def solution(mesh):
    return jax.shard_map(
        per_device,
        mesh=mesh,
        in_specs=(P("grp", "blk"), P("grp", "blk"), P("grp", "blk")),
        out_specs=P("grp", "blk"),
        check_vma=False,
    )
```
